512 devices in a mesh: replica: 32 (over y, z_hi), mp: 16 (over z_lo, x, core).
Axes of the slice: x: 4, y: 8, z: 8 (z_hi: 4, z_lo: 2; z = z_hi * 2 + z_lo), core: 2. Of those that a mesh axis runs over, the one named last changes fastest.
Arguments:
- inputs: bfloat16 [32, 384, 4608], P('replica', 'mp'), may hold values from -10 to 10
- out_grads: bfloat16 [32, 384, 4608], P('replica', 'mp'), may hold values from -6 to 6
- norm_gain: float32 [4608], replicated, may hold values from 0.5 to 1.5
- doc_ids: int32 [32, 384], P('replica'), may hold values from 0 to 3, never falling along the last dimension, each value on 1 to 192 neighbouring positions
- w_query: bfloat16 [32, 4608, 2048], P('replica', None, 'mp'), may hold values from -9 to 9
- w_keyval: bfloat16 [32, 4608, 2048], P('replica', None, 'mp'), may hold values from -9 to 9
- w_out: bfloat16 [32, 2048, 4608], P('replica', 'mp'), may hold values from -6 to 6
- outer_params: float32 [16, 128, 4608], P('mp', 'replica'), may hold values from -6 to 6
- outer_moment: float32 [16, 128, 4608], P('mp', 'replica'), may hold values from -6 to 6
Outputs:
- input_grads: bfloat16 [32, 384, 4608], P('replica', 'mp')
- new_params: float32 [16, 128, 4608], P('mp', 'replica')
- new_moment: float32 [16, 128, 4608], P('mp', 'replica')
The draws below stay inside these ranges and needn't reach their ends.
All inputs are finite; a program needn't handle non-finite values.
Results may differ from the reference program's by a relative error of at most 0.018.
Values may be sent and summed in bfloat16 or wider, within the bound.
A program may use at most 64 MiB of HBM per device.

```python
import math
import jax
import jax.numpy as jnp
import numpy as np
from jax import lax

D = 4608
HEAD_DIM = 128
SEQ = 384
HEADS = 16
KV_HEADS = 8
REPLICAS = 32
N_REPLICA = 32


def draw_inputs(key, part):
    key = jax.random.fold_in(key, 1)
    noise_key = jax.random.fold_in(key, 0)
    values = jnp.clip(jax.random.normal(noise_key, (REPLICAS, SEQ, D), jnp.float32), -6.0, 6.0)
    return values.astype(jnp.bfloat16)


def draw_w_query(key, part):
    key = jax.random.fold_in(key, 2)
    noise_key = jax.random.fold_in(key, 0)
    values = jnp.clip(jax.random.normal(noise_key, (REPLICAS, D, HEADS * HEAD_DIM), jnp.float32), -6.0, 6.0)
    return values.astype(jnp.bfloat16)


def draw_w_keyval(key, part):
    key = jax.random.fold_in(key, 3)
    noise_key = jax.random.fold_in(key, 0)
    values = jnp.clip(jax.random.normal(noise_key, (REPLICAS, D, HEADS * HEAD_DIM), jnp.float32), -6.0, 6.0)
    return values.astype(jnp.bfloat16)


def level_of(stream_key, dims, shards, smallest, top_value):
    factor_of, own = 1.0, jax.random.fold_in(stream_key, 6)
    for position, blocks in shards:
        steps = jnp.exp(jax.random.uniform(jax.random.fold_in(own, position), (blocks,), jnp.float32, smallest / len(shards), top_value / len(shards)))
        factor_of = factor_of * jnp.repeat(steps, dims[position] // blocks).reshape([-1 if axis == position else 1 for axis in range(len(dims))])
    return factor_of


def profile(amount, total, bound, skew):
    weights = [(1 << 20) // math.isqrt(grade ** skew) + 1 for grade in range(2, amount + 1)]
    surplus, holding = total - bound - (amount - 1), [1] * (amount - 1)
    while surplus > 0:
        movable = [i for i in range(amount - 1) if holding[i] < bound]
        whole, budget = sum([weights[i] for i in movable]), surplus
        for i in movable:
            extra = min(bound - holding[i], max(1, budget * weights[i] // whole), surplus)
            holding[i] = holding[i] + extra
            surplus = surplus - extra
    return np.array([bound] + holding)


def uneven_parts(key, amount, total, most, skew):
    if amount == 2:
        one = jax.random.randint(key, (), max(1, total - most), min(most, total - 1) + 1)
        return jnp.stack([one, total - one])
    tallies = jnp.asarray(profile(amount, total, most, skew), jnp.int32)
    twos = (amount - 1) // 2
    giver, sink = tallies[1:1 + 2 * twos:2], tallies[2:2 + 2 * twos:2]
    slack = jnp.minimum(giver - 1, most - sink)
    moved = jax.random.randint(jax.random.fold_in(key, 1), (twos,), 0, 1 << 20) % (slack + 1)
    tallies = tallies.at[1:1 + 2 * twos:2].set(giver - moved).at[2:2 + 2 * twos:2].set(sink + moved)
    return tallies[jax.random.permutation(jax.random.fold_in(key, 2), amount)]


def gaussian(rng, shape, deviation, most, pieces=(), kind=jnp.bfloat16):
    values = deviation * jax.random.normal(rng, shape, jnp.float32)
    if pieces:
        values = values * level_of(rng, shape, pieces, -0.22, 0.18)
    return jnp.clip(values, -most, most).astype(kind)


def setup_inputs(seed: int = 0) -> dict:
    splits = jax.random.split(jax.random.key(seed), 10)
    inputs = draw_inputs(jax.random.fold_in(splits[9], 71), 0)
    out_grads = gaussian(splits[1], (REPLICAS, SEQ, D), 1.0, 6.0, ((0, 32), (1, 16)))
    norm_gain = jnp.clip(1.0 + 0.1 * jax.random.normal(splits[2], (D,), jnp.float32), 0.5, 1.5)
    doc_ids = jax.vmap(lambda own: jnp.searchsorted(jnp.cumsum(uneven_parts(own, 4, SEQ, SEQ // 2, 0)), jnp.arange(SEQ), side="right"))(jax.random.split(splits[3], REPLICAS)).reshape((REPLICAS, SEQ)).astype(jnp.int32)
    w_query = draw_w_query(jax.random.fold_in(splits[9], 71), 0)
    w_keyval = draw_w_keyval(jax.random.fold_in(splits[9], 71), 0)
    w_out = gaussian(splits[6], (REPLICAS, HEADS * HEAD_DIM, D), 1.0, 6.0, ((0, 32), (1, 16)))
    outer_params = gaussian(splits[7], (HEADS, HEAD_DIM, D), 1.0, 6.0, ((0, 16), (1, 32)), jnp.float32)
    outer_moment = gaussian(splits[8], (HEADS, HEAD_DIM, D), 1.0, 6.0, ((0, 16), (1, 32)), jnp.float32)
    return dict(inputs=inputs, out_grads=out_grads, norm_gain=norm_gain, doc_ids=doc_ids, w_query=w_query, w_keyval=w_keyval, w_out=w_out, outer_params=outer_params, outer_moment=outer_moment)


def replica_grads(inputs_r, grads_r, docs_r, query_r, keyval_r, out_r, norm_gain):
    seq_len = inputs_r.shape[0]
    width_scale = D ** (-0.5)
    score_scale = 144.0 ** (-0.5)
    out_scale = (HEADS * HEAD_DIM) ** (-0.5)
    inputs_float = inputs_r.astype(jnp.float32)
    inv_rms = lax.rsqrt(lax.optimization_barrier(jnp.mean(inputs_float * inputs_float, axis=-1, keepdims=True)) + 1e-06)
    normed = (inputs_float * inv_rms * norm_gain).astype(jnp.bfloat16)
    queries = (jnp.dot(normed, query_r, preferred_element_type=jnp.float32) * width_scale).astype(jnp.bfloat16)
    queries = queries.reshape(seq_len, HEADS, HEAD_DIM)
    keyval = (jnp.dot(normed, keyval_r, preferred_element_type=jnp.float32) * width_scale).astype(jnp.bfloat16)
    keyval = keyval.reshape(seq_len, KV_HEADS, 2, HEAD_DIM)
    keys_heads = jnp.repeat(keyval[:, :, 0], 2, axis=1)
    values_heads = jnp.repeat(keyval[:, :, 1], 2, axis=1)
    positions = jnp.arange(seq_len)
    allowed_pairs = (positions[None, :] <= positions[:, None]) & (docs_r[:, None] == docs_r[None, :])
    scores = jnp.einsum('shd,thd->hst', queries.astype(jnp.float32), keys_heads.astype(jnp.float32)) * score_scale
    scores = jnp.where(allowed_pairs[None], scores, -1e+30)
    probs = jax.nn.softmax(scores, axis=-1)
    probs_low = probs.astype(jnp.bfloat16)
    head_grads = (jnp.dot(grads_r, out_r.T, preferred_element_type=jnp.float32) * out_scale).astype(jnp.bfloat16)
    head_grads = head_grads.reshape(seq_len, HEADS, HEAD_DIM)
    prob_grads = jnp.einsum('shd,thd->hst', head_grads.astype(jnp.float32), values_heads.astype(jnp.float32))
    score_grads = probs * (prob_grads - lax.optimization_barrier(jnp.sum(probs * prob_grads, axis=-1, keepdims=True))) * score_scale
    score_grads = score_grads.astype(jnp.bfloat16)
    query_grads = jnp.einsum('hst,thd->shd', score_grads.astype(jnp.float32), keys_heads.astype(jnp.float32)).astype(jnp.bfloat16)
    key_parts = jnp.einsum('hst,shd->thd', score_grads.astype(jnp.float32), queries.astype(jnp.float32)).astype(jnp.bfloat16)
    value_parts = jnp.einsum('hst,shd->thd', probs_low.astype(jnp.float32), head_grads.astype(jnp.float32)).astype(jnp.bfloat16)
    key_grads = lax.optimization_barrier(jnp.sum(key_parts.astype(jnp.float32).reshape(seq_len, KV_HEADS, 2, HEAD_DIM), axis=2)).astype(jnp.bfloat16)
    value_grads = lax.optimization_barrier(jnp.sum(value_parts.astype(jnp.float32).reshape(seq_len, KV_HEADS, 2, HEAD_DIM), axis=2)).astype(jnp.bfloat16)
    keyval_grads = jnp.stack([key_grads, value_grads], axis=2).reshape(seq_len, HEADS, HEAD_DIM)
    query_heads = query_r.reshape(D, HEADS, HEAD_DIM).astype(jnp.float32)
    keyval_heads = keyval_r.reshape(D, HEADS, HEAD_DIM).astype(jnp.float32)
    head_terms = jnp.einsum('shd,ehd->hse', query_grads.astype(jnp.float32), query_heads)
    head_terms = head_terms + jnp.einsum('shd,ehd->hse', keyval_grads.astype(jnp.float32), keyval_heads)
    head_terms = lax.optimization_barrier((head_terms * width_scale).astype(jnp.bfloat16))
    normed_grads = lax.optimization_barrier(jnp.sum(head_terms.astype(jnp.float32), axis=0))
    scaled = normed_grads * norm_gain
    centered = inputs_float * inv_rms
    result = grads_r.astype(jnp.float32) + inv_rms * (scaled - centered * lax.optimization_barrier(jnp.mean(scaled * centered, axis=-1, keepdims=True)))
    return result.astype(jnp.bfloat16)

def reference(inputs, out_grads, norm_gain, doc_ids, w_query, w_keyval, w_out, outer_params, outer_moment):

    def one_replica(items):
        return replica_grads(items[0], items[1], items[2], items[3], items[4], items[5], norm_gain)
    input_grads = lax.map(one_replica, (inputs, out_grads, doc_ids, w_query, w_keyval, w_out))
    local_mean = lax.optimization_barrier(jnp.sum(w_out, axis=0, dtype=jnp.float32)).reshape(HEADS, HEAD_DIM, D) / N_REPLICA
    delta = outer_params - local_mean
    new_moment = 0.9 * outer_moment + delta
    new_params = outer_params - 0.7 * (delta + 0.9 * new_moment)
    return (input_grads, new_params, new_moment)
```

```python
import jax
import jax.numpy as jnp
from jax import lax
from jax.experimental import pallas as pl
from jax.experimental.pallas import tpu as pltpu
from jax.sharding import PartitionSpec as P

D = 4608
HEAD_DIM = 128
SEQ = 384
ROWS = 24
HALF = 192
GATHER = 6
GW = D // GATHER
SUMS = 9
SW = D // SUMS
Y_SIZE = 8
Z_HI = 4
OUTER_ROWS = 4
N_REPLICA = 32
MESH = pl.DeviceIdType.MESH
F32 = jnp.float32
BF16 = jnp.bfloat16
CONTRACT_LAST = (((1,), (1,)), ((), ()))
CONTRACT_FIRST = (((0,), (0,)), ((), ()))
MAX_SENDS = 192
SUM_PLAN = (
    ("z", 1), ("x", 0), ("z", 1), ("x", 1), ("z", 1), ("x", 0), ("z", 0), ("x", 1), ("x", 0),
)


def kernel(
    inputs, out_grads, gain, docs, w_query, w_keyval, w_out, outer_params, outer_moment,
    input_grads, new_params, new_moment,
    normed_all, grads_all, w_in, w_back, bias, acc_in, acc_back, heads, heads_out,
    back, back_out, back_in, grad_rows, terms, hop_x, near_x, hop_z, near_z, from_z_x, from_z_z,
    totals, relay, far, y_in, z_out, z_in, send_sems, recv_sems, local_sems,
):
    width_scale = D ** (-0.5)
    score_scale = 144.0 ** (-0.5)
    out_scale = (16 * HEAD_DIM) ** (-0.5)
    replica = lax.axis_index("replica")
    model = lax.axis_index("mp")
    c = lax.rem(model, 2)
    x = lax.rem(lax.div(model, 2), 4)
    z = lax.div(model, 8)
    y = lax.div(replica, Z_HI)
    zh = lax.rem(replica, Z_HI)
    other_c = 1 - c
    other_z = 1 - z
    x_at = [lax.rem(x + i, 4) for i in range(4)]

    def on_model(zz, xx, cc):
        return (replica, (zz * 4 + xx) * 2 + cc)

    right = on_model(z, x_at[1], c)
    left = on_model(z, x_at[3], c)
    across = on_model(other_z, x, c)
    sibling = on_model(z, x, other_c)
    sides = (right, left)

    def y_device(distance):
        return (lax.rem(y + distance + Y_SIZE, Y_SIZE) * Z_HI + zh, model)

    def z_device(distance):
        return (y * Z_HI + lax.rem(zh + distance, Z_HI), model)

    partners = [right, left, across, sibling]
    partners += [y_device(d) for d in (1, -1, 2, -2, 3, -3)]
    partners += [z_device(d) for d in (1, 2, 3)]
    barrier = pltpu.get_barrier_semaphore()
    for partner in partners:
        pl.semaphore_signal(barrier, inc=1, device_id=partner, device_id_type=MESH)

    sent = []

    def send(src, dst, device):
        index = len(sent)
        assert index < MAX_SENDS
        copy = pltpu.make_async_remote_copy(
            src_ref=src, dst_ref=dst, send_sem=send_sems.at[index], recv_sem=recv_sems.at[index],
            device_id=device, device_id_type=MESH,
        )
        copy.start()
        sent.append(copy)
        return copy

    own_columns = pl.ds(pl.multiple_of(c * HEAD_DIM, HEAD_DIM), HEAD_DIM)
    own_keyval = pl.ds(pl.multiple_of(2 * HEAD_DIM + c * HEAD_DIM, HEAD_DIM), HEAD_DIM)
    weight_moves = (
        (w_out, w_back.at[own_columns, :]),
        (w_query, w_in.at[:, own_columns]),
        (w_keyval, w_in.at[:, own_keyval]),
    )
    local = []
    for index, (src, dst) in enumerate(weight_moves):
        copy = pltpu.make_async_copy(src, dst, local_sems.at[index])
        copy.start()
        local.append(copy)

    rows = inputs[...].astype(F32)
    inv_rms = lax.rsqrt(jnp.sum(rows * rows, axis=-1, keepdims=True) * (1.0 / D) + 1e-06)
    normed_all[z, x] = (rows * inv_rms * gain[...]).astype(BF16)
    grads_all[z, x] = out_grads[...]

    pl.semaphore_wait(barrier, len(partners))

    def columns(k):
        return pl.ds(k * GW, GW)

    def normed_part(zz, xx, k):
        return normed_all.at[zz, xx, :, columns(k)]

    def grads_part(zz, xx, k):
        return grads_all.at[zz, xx, :, columns(k)]

    chunks = range(GATHER)
    grads_across, normed_near, normed_across = [], [], []
    for k in chunks:
        part = grads_part(z, x, k)
        grads_across.append(send(part, part, across))
        part = normed_part(z, x, k)
        normed_near.append([send(part, part, side) for side in sides])
    for k in chunks:
        part = normed_part(z, x, k)
        normed_across.append([send(part, part, across)])

    def y_rows(distance, base=0):
        owner = lax.rem(y + distance + Y_SIZE, Y_SIZE)
        return pl.ds(pl.multiple_of(base + owner * 16, 16), 16)

    half_columns = (pl.ds(0, D // 2), pl.ds(D // 2, D // 2))
    relays = []
    for i, distance in enumerate((1, -1)):
        relays.append(
            send(w_out.at[y_rows(4), half_columns[i]], relay.at[i], y_device(distance))
        )
    weights = [send(src, dst, sibling) for src, dst in weight_moves]
    y_moves = []
    for i, distance in enumerate((1, -1, 2, -2)):
        y_moves.append(send(w_out.at[y_rows(distance), :], y_in.at[i], y_device(distance)))

    row_at = lax.broadcasted_iota(jnp.int32, (SEQ, SEQ), 0)
    column_at = lax.broadcasted_iota(jnp.int32, (SEQ, SEQ), 1)
    documents = jnp.broadcast_to(docs[...].astype(F32), (SEQ, SEQ))
    own_document = jnp.sum(
        jnp.where(row_at == column_at, documents, 0.0), axis=-1, keepdims=True
    )
    allowed = (column_at <= row_at) & (documents == own_document)
    bias[...] = jnp.where(allowed, 0.0, -1e30)

    normed_far, grads_near = [], []
    for k in chunks:
        for i, (side, slot) in enumerate(((right, 3), (left, 1))):
            normed_near[k][i].wait_recv()
            part = normed_part(z, x_at[slot], k)
            if k % 2 == i:
                normed_far.append(send(part, part, side))
            normed_across[k].append(send(part, part, across))
        grads_across[k].wait_recv()
        part = grads_all.at[:, x, :, columns(k)]
        grads_near.append([send(part, part, side) for side in sides])

    for copy in local:
        copy.wait()
    for copy in weights:
        copy.wait_recv()
    for i, distance in enumerate((3, -3)):
        relays[i].wait_recv()
        far[i] = w_back[y_rows(distance, c * HEAD_DIM), :]
        far[i, :, half_columns[i]] = (
            far[i, :, half_columns[i]].astype(F32) + relay[i].astype(F32)
        ).astype(BF16)
        y_moves.append(send(far.at[i], y_in.at[4 + i], y_device(distance)))

    for k in chunks:
        normed_far[k].wait_recv()
        part = normed_part(z, x_at[2], k)
        normed_across[k].append(send(part, part, across))
    grads_far = []
    for k in chunks:
        for i, (side, slot) in enumerate(((right, 3), (left, 1))):
            grads_near[k][i].wait_recv()
            if k % 2 == i:
                part = grads_all.at[:, x_at[slot], :, columns(k)]
                grads_far.append(send(part, part, side))

    acc_back[...] = jnp.zeros_like(acc_back)
    acc_in[...] = jnp.zeros_like(acc_in)
    for k in chunks:
        grads_far[k].wait_recv()
        acc_back[...] += lax.dot_general(
            grads_all[:, :, :, columns(k)].reshape(HALF, GW), w_back[:, columns(k)],
            CONTRACT_LAST, preferred_element_type=F32,
        )
    for k in chunks:
        for copy in normed_across[k]:
            copy.wait_recv()
        acc_in[...] += jnp.dot(
            normed_all[:, :, :, columns(k)].reshape(HALF, GW), w_in[columns(k), :],
            preferred_element_type=F32,
        )

    def blocks(value):
        return value.reshape(8, ROWS, HEAD_DIM)

    first = c == 0

    def column_block(ref, i):
        return ref[:, i * HEAD_DIM : (i + 1) * HEAD_DIM]

    queries = [blocks(column_block(acc_in, i) * width_scale).astype(BF16) for i in range(2)]
    head_grads = [blocks(column_block(acc_back, i) * out_scale).astype(BF16) for i in range(2)]
    keyval = [blocks(column_block(acc_in, i) * width_scale).astype(BF16) for i in (2, 3)]

    def pick(pair, condition):
        return jnp.where(condition, pair[0].astype(F32), pair[1].astype(F32)).astype(BF16)

    heads_out[0] = pick(queries, ~first)
    heads_out[1] = pick(head_grads, ~first)
    heads_out[2] = keyval[0]
    heads_out[3] = keyval[1]
    exchange = send(heads_out, heads.at[:, :, c], sibling)
    heads[0, :, c] = pick(queries, first)
    heads[1, :, c] = pick(head_grads, first)
    heads[2, :, c] = keyval[0]
    heads[3, :, c] = keyval[1]
    exchange.wait_recv()

    def sequence(i):
        return heads[i].astype(F32).reshape(SEQ, HEAD_DIM).astype(BF16)

    query, head_grad, key, value = [sequence(i) for i in range(4)]
    key_parts, value_parts = [None] * 3, [None] * 3
    for i in range(3):
        limit = (i + 1) * 128
        here = slice(i * 128, limit)
        scores = lax.dot_general(
            query[here], key[:limit], CONTRACT_LAST, preferred_element_type=F32
        )
        scores = scores * score_scale + bias[here, :limit]
        powers = jnp.exp(scores - jnp.max(scores, axis=-1, keepdims=True))
        probs = powers / jnp.sum(powers, axis=-1, keepdims=True)
        prob_grads = lax.dot_general(
            head_grad[here], value[:limit], CONTRACT_LAST, preferred_element_type=F32
        )
        score_grads = (
            probs
            * (prob_grads - jnp.sum(probs * prob_grads, axis=-1, keepdims=True))
            * score_scale
        ).astype(BF16)
        probs_low = probs.astype(BF16)
        query_grads = jnp.dot(score_grads, key[:limit], preferred_element_type=F32)
        grad_rows[0, here] = query_grads
        for j in range(i + 1):
            there = slice(j * 128, (j + 1) * 128)
            key_term = lax.dot_general(
                score_grads[:, there], query[here], CONTRACT_FIRST, preferred_element_type=F32
            )
            value_term = lax.dot_general(
                probs_low[:, there], head_grad[here], CONTRACT_FIRST, preferred_element_type=F32
            )
            key_parts[j] = key_term if i == j else key_parts[j] + key_term
            value_parts[j] = value_term if i == j else value_parts[j] + value_term
    for j in range(3):
        there = slice(j * 128, (j + 1) * 128)
        grad_rows[1, there] = key_parts[j]
        grad_rows[2, there] = value_parts[j]
    for i in range(3):
        back[i] = grad_rows[i].reshape(8, 2, ROWS, HEAD_DIM).astype(BF16)
    exchange_back = send(back.at[:, :, other_c], back_in, sibling)

    for copy in y_moves:
        copy.wait_recv()
    total = w_back[y_rows(0, c * HEAD_DIM), :].astype(F32)
    for i in range(6):
        total = total + y_in[i].astype(F32)
    totals[...] = total
    for i in range(Z_HI):
        z_out[i] = totals[i * OUTER_ROWS : (i + 1) * OUTER_ROWS, :].astype(BF16)
    z_moves = []
    for distance in (1, 2, 3):
        owner = lax.rem(zh + distance, Z_HI)
        z_moves.append(send(z_out.at[owner], z_in.at[distance - 1], z_device(distance)))

    exchange_back.wait_recv()

    def own_rows(i):
        return back[i, :, c].astype(F32).reshape(HALF, HEAD_DIM)

    def received_rows(i):
        return back_in[i].astype(F32).reshape(HALF, HEAD_DIM)

    query_pair = (own_rows(0), received_rows(0))
    upstream = jnp.concatenate(
        [
            jnp.where(first, query_pair[0], query_pair[1]).astype(BF16),
            jnp.where(first, query_pair[1], query_pair[0]).astype(BF16),
            (own_rows(1) + received_rows(1)).astype(BF16),
            (own_rows(2) + received_rows(2)).astype(BF16),
        ],
        axis=1,
    )

    def sum_columns(j):
        return pl.ds(j * SW, SW)

    hops, nears, across_moves = {}, {}, {}
    plan = list(enumerate(SUM_PLAN))
    by_x = [(j, way) for j, (kind, way) in plan if kind == "x"]
    by_z = [(j, way) for j, (kind, way) in plan if kind == "z"]
    forward_slot = {0: 1, 1: 3}
    for j, (kind, way) in plan:
        term = lax.dot_general(
            upstream, w_in[sum_columns(j), :], CONTRACT_LAST, preferred_element_type=F32
        )
        terms[:, :, :, sum_columns(j)] = (
            (term * width_scale).reshape(2, 4, ROWS, SW).astype(BF16)
        )
        if kind == "z":
            across_moves[j] = send(
                terms.at[other_z, :, :, sum_columns(j)], from_z_z.at[len(across_moves)], across
            )
        else:
            slot = len(hops)
            forward, backward = forward_slot[way], forward_slot[1 - way]
            hops[j] = send(
                terms.at[:, x_at[2], :, sum_columns(j)], hop_x.at[slot], sides[way]
            )
            nears[j] = [
                send(
                    terms.at[:, x_at[backward], :, sum_columns(j)], near_x.at[slot, 0],
                    sides[1 - way],
                )
            ]

    for slot, (j, way) in enumerate(by_x):
        forward = forward_slot[way]
        hops[j].wait_recv()
        terms[:, x_at[forward], :, sum_columns(j)] = (
            terms[:, x_at[forward], :, sum_columns(j)].astype(F32) + hop_x[slot].astype(F32)
        ).astype(BF16)
        nears[j].append(
            send(
                terms.at[:, x_at[forward], :, sum_columns(j)], near_x.at[slot, 1], sides[way]
            )
        )
    for slot, (j, way) in enumerate(by_z):
        forward, backward = forward_slot[way], forward_slot[1 - way]
        across_moves[j].wait_recv()
        terms[z, :, :, sum_columns(j)] = (
            terms[z, :, :, sum_columns(j)].astype(F32) + from_z_z[slot].astype(F32)
        ).astype(BF16)
        hops[j] = send(terms.at[z, x_at[2], :, sum_columns(j)], hop_z.at[slot], sides[way])
        nears[j] = [
            send(
                terms.at[z, x_at[backward], :, sum_columns(j)], near_z.at[slot, 0],
                sides[1 - way],
            )
        ]
    for slot, (j, way) in enumerate(by_x):
        for copy in nears[j]:
            copy.wait_recv()
        terms[:, x, :, sum_columns(j)] = (
            terms[:, x, :, sum_columns(j)].astype(F32)
            + near_x[slot, 0].astype(F32)
            + near_x[slot, 1].astype(F32)
        ).astype(BF16)
        across_moves[j] = send(
            terms.at[other_z, x, :, sum_columns(j)], from_z_x.at[slot], across
        )
    for slot, (j, way) in enumerate(by_z):
        forward = forward_slot[way]
        hops[j].wait_recv()
        terms[z, x_at[forward], :, sum_columns(j)] = (
            terms[z, x_at[forward], :, sum_columns(j)].astype(F32) + hop_z[slot].astype(F32)
        ).astype(BF16)
        nears[j].append(
            send(
                terms.at[z, x_at[forward], :, sum_columns(j)], near_z.at[slot, 1], sides[way]
            )
        )

    for copy in z_moves:
        copy.wait_recv()
    mean = z_out[zh].astype(F32)
    for i in range(3):
        mean = mean + z_in[i].astype(F32)
    mean = mean * (1.0 / N_REPLICA)
    delta = outer_params[...] - mean
    moment = 0.9 * outer_moment[...] + delta
    new_moment[...] = moment
    new_params[...] = outer_params[...] - 0.7 * (delta + 0.9 * moment)

    normed_grads = [None] * SUMS
    for slot, (j, way) in enumerate(by_x):
        across_moves[j].wait_recv()
        normed_grads[j] = terms[z, x, :, sum_columns(j)].astype(F32) + from_z_x[slot].astype(F32)
    for slot, (j, way) in enumerate(by_z):
        for copy in nears[j]:
            copy.wait_recv()
        normed_grads[j] = (
            terms[z, x, :, sum_columns(j)].astype(F32)
            + near_z[slot, 0].astype(F32)
            + near_z[slot, 1].astype(F32)
        )
    scaled = jnp.concatenate(normed_grads, axis=1) * gain[...]
    centered = inputs[...].astype(F32) * inv_rms
    projected = jnp.sum(scaled * centered, axis=-1, keepdims=True) * (1.0 / D)
    input_grads[...] = (
        out_grads[...].astype(F32) + inv_rms * (scaled - centered * projected)
    ).astype(BF16)
    for copy in sent:
        copy.wait_send()


def on_device(
    inputs, out_grads, norm_gain, doc_ids, w_query, w_keyval, w_out, outer_params, outer_moment
):
    vmem = pl.BlockSpec(memory_space=pltpu.VMEM)
    anywhere = pl.BlockSpec(memory_space=pl.ANY)
    by_x = sum(kind == "x" for kind, _ in SUM_PLAN)
    by_z = SUMS - by_x
    input_grads, new_params, new_moment = pl.pallas_call(
        kernel,
        out_shape=(
            jax.ShapeDtypeStruct((ROWS, D), BF16),
            jax.ShapeDtypeStruct((OUTER_ROWS, D), F32),
            jax.ShapeDtypeStruct((OUTER_ROWS, D), F32),
        ),
        in_specs=[vmem, vmem, vmem, vmem, anywhere, anywhere, anywhere, vmem, vmem],
        out_specs=(vmem, vmem, vmem),
        scratch_shapes=[
            pltpu.VMEM((2, 4, ROWS, D), BF16),
            pltpu.VMEM((2, 4, ROWS, D), BF16),
            pltpu.VMEM((D, 4 * HEAD_DIM), BF16),
            pltpu.VMEM((2 * HEAD_DIM, D), BF16),
            pltpu.VMEM((SEQ, SEQ), F32),
            pltpu.VMEM((HALF, 4 * HEAD_DIM), F32),
            pltpu.VMEM((HALF, 2 * HEAD_DIM), F32),
            pltpu.VMEM((4, 8, 2, ROWS, HEAD_DIM), BF16),
            pltpu.VMEM((4, 8, ROWS, HEAD_DIM), BF16),
            pltpu.VMEM((3, 8, 2, ROWS, HEAD_DIM), BF16),
            pltpu.VMEM((3, 8, ROWS, HEAD_DIM), BF16),
            pltpu.VMEM((3, 8, ROWS, HEAD_DIM), BF16),
            pltpu.VMEM((3, SEQ, HEAD_DIM), F32),
            pltpu.VMEM((2, 4, ROWS, D), BF16),
            pltpu.VMEM((by_x, 2, ROWS, SW), BF16),
            pltpu.VMEM((by_x, 2, 2, ROWS, SW), BF16),
            pltpu.VMEM((by_z, ROWS, SW), BF16),
            pltpu.VMEM((by_z, 2, ROWS, SW), BF16),
            pltpu.VMEM((by_x, ROWS, SW), BF16),
            pltpu.VMEM((by_z, 4, ROWS, SW), BF16),
            pltpu.VMEM((16, D), F32),
            pltpu.VMEM((2, 16, D // 2), BF16),
            pltpu.VMEM((2, 16, D), BF16),
            pltpu.VMEM((6, 16, D), BF16),
            pltpu.VMEM((Z_HI, OUTER_ROWS, D), BF16),
            pltpu.VMEM((Z_HI - 1, OUTER_ROWS, D), BF16),
            pltpu.SemaphoreType.DMA((MAX_SENDS,)),
            pltpu.SemaphoreType.DMA((MAX_SENDS,)),
            pltpu.SemaphoreType.DMA((3,)),
        ],
        compiler_params=pltpu.CompilerParams(
            collective_id=0, has_side_effects=True, vmem_limit_bytes=48 * 2**20
        ),
        name="layer_backward",
    )(
        inputs[0], out_grads[0], norm_gain[None], doc_ids, w_query[0], w_keyval[0], w_out[0],
        outer_params[0], outer_moment[0],
    )
    return input_grads[None], new_params[None], new_moment[None]


def solution(mesh):
    placed = (
        P("replica", "mp", None),
        P("replica", "mp", None),
        P(),
        P("replica", None),
        P("replica", None, "mp"),
        P("replica", None, "mp"),
        P("replica", "mp", None),
        P("mp", "replica", None),
        P("mp", "replica", None),
    )
    return jax.shard_map(
        on_device,
        mesh=mesh,
        in_specs=placed,
        out_specs=(P("replica", "mp", None), P("mp", "replica", None), P("mp", "replica", None)),
        check_vma=False,
    )
```

```python
import jax
import jax.numpy as jnp
from jax import lax
from jax.experimental import pallas as pl
from jax.experimental.pallas import tpu as pltpu
from jax.sharding import PartitionSpec as P

D = 4608
HEAD_DIM = 128
SEQ = 384
ROWS = 24
HALF = 192
GATHER = 6
GW = D // GATHER
SUMS = 9
SW = D // SUMS
Y_SIZE = 8
Z_HI = 4
OUTER_ROWS = 4
N_REPLICA = 32
MESH = pl.DeviceIdType.MESH
F32 = jnp.float32
BF16 = jnp.bfloat16
CONTRACT_LAST = (((1,), (1,)), ((), ()))
CONTRACT_FIRST = (((0,), (0,)), ((), ()))
N_RECEIVE = 72
N_SEND = 7
N_LOCAL = 8
SUM_PLAN = (
    ("z", 1), ("x", 0), ("z", 1), ("x", 1), ("z", 1), ("x", 0), ("z", 0), ("x", 1), ("x", 0),
)


def kernel(
    inputs_hbm, out_grads_hbm, gain_hbm, docs_hbm, w_query, w_keyval, w_out, params_hbm, moment_hbm,
    input_grads, new_params, new_moment,
    inputs, out_grads, gain, docs, outer_params, outer_moment,
    normed_all, grads_all, w_in, w_back, bias, acc_in, acc_back, heads, heads_out,
    back, back_out, back_in, grad_rows, terms, hop_x, near_x, hop_z, near_z, from_z_x, from_z_z,
    totals, relay, far, y_in, z_out, up_in, up_out, down_in, down_out, mine,
    send_sems, recv_sems, local_sems,
):
    width_scale = D ** (-0.5)
    score_scale = 144.0 ** (-0.5)
    out_scale = (16 * HEAD_DIM) ** (-0.5)
    replica = lax.axis_index("replica")
    model = lax.axis_index("mp")
    c = lax.rem(model, 2)
    x = lax.rem(lax.div(model, 2), 4)
    z = lax.div(model, 8)
    y = lax.div(replica, Z_HI)
    zh = lax.rem(replica, Z_HI)
    other_c = 1 - c
    other_z = 1 - z
    x_at = [lax.rem(x + i, 4) for i in range(4)]

    def on_model(zz, xx, cc):
        return (replica, (zz * 4 + xx) * 2 + cc)

    right = on_model(z, x_at[1], c)
    left = on_model(z, x_at[3], c)
    across = on_model(other_z, x, c)
    sibling = on_model(z, x, other_c)
    sides = (right, left)

    def y_device(distance):
        return (lax.rem(y + distance + Y_SIZE, Y_SIZE) * Z_HI + zh, model)

    def z_device(distance):
        return (replica + distance, model)

    partners = [right, left, across, sibling]
    partners += [y_device(d) for d in (1, -1, 2, -2, 3, -3)]
    barrier = pltpu.get_barrier_semaphore()
    for partner in partners:
        pl.semaphore_signal(barrier, inc=1, device_id=partner, device_id_type=MESH)
    line_steps = ((zh < Z_HI - 1, 1), (zh > 0, -1))
    for has_neighbour, step in line_steps:

        @pl.when(has_neighbour)
        def _():
            pl.semaphore_signal(
                barrier, inc=1, device_id=z_device(step), device_id_type=MESH
            )

    own_columns = pl.ds(pl.multiple_of(c * HEAD_DIM, HEAD_DIM), HEAD_DIM)
    own_keyval = pl.ds(pl.multiple_of(2 * HEAD_DIM + c * HEAD_DIM, HEAD_DIM), HEAD_DIM)
    weight_moves = (
        (w_out, w_back.at[own_columns, :]),
        (w_query, w_in.at[:, own_columns]),
        (w_keyval, w_in.at[:, own_keyval]),
    )
    moves = (
        (inputs_hbm, inputs),
        (gain_hbm, gain.at[0]),
        (out_grads_hbm, grads_all.at[z, x]),
        (docs_hbm, docs),
        (out_grads_hbm, out_grads),
        (params_hbm, outer_params),
        (moment_hbm, outer_moment),
    ) + weight_moves
    local = []
    for index, (src, dst) in enumerate(moves):
        copy = pltpu.make_async_copy(src, dst, local_sems.at[min(index, N_LOCAL - 1)])
        copy.start()
        local.append(copy)

    receivers = iter(range(N_RECEIVE))

    def receiver():
        return recv_sems.at[next(receivers)]

    def send(src, dst, device, arrival, group=0):
        copy = pltpu.make_async_remote_copy(
            src_ref=src, dst_ref=dst, send_sem=send_sems.at[group], recv_sem=arrival,
            device_id=device, device_id_type=MESH,
        )
        copy.start()

    def wait_bytes_of(ref, semaphore):
        pltpu.make_async_copy(ref, ref, semaphore).wait()

    local[0].wait()
    rows = inputs[...].astype(F32)
    inv_rms = lax.rsqrt(jnp.sum(rows * rows, axis=-1, keepdims=True) * (1.0 / D) + 1e-06)
    local[1].wait()
    normed_all[z, x] = (rows * inv_rms * gain[...]).astype(BF16)
    local[2].wait()

    line_neighbours = 1 + lax.rem(lax.div(zh + 1, 2), 2)
    pl.semaphore_wait(barrier, len(partners) + line_neighbours)

    def columns(k):
        return pl.ds(k * GW, GW)

    def normed_part(zz, xx, k):
        return normed_all.at[zz, xx, :, columns(k)]

    def grads_part(zz, xx, k):
        return grads_all.at[zz, xx, :, columns(k)]

    chunks = range(GATHER)
    z_first = GATHER - 1
    grads_crossed, grads_near, grads_far = [[receiver() for _ in chunks] for _ in range(3)]
    normed_near, normed_far, normed_crossed = [[receiver() for _ in chunks] for _ in range(3)]
    for k in chunks:
        part = grads_part(z, x, k)
        send(part, part, across, grads_crossed[k])
        part = normed_part(z, x, k)
        for side in sides:
            send(part, part, side, normed_near[k])
    for k in chunks:
        part = normed_part(z, x, k)
        send(part, part, across, normed_crossed[k])

    def y_rows(distance, base=0):
        owner = lax.rem(y + distance + Y_SIZE, Y_SIZE)
        return pl.ds(pl.multiple_of(base + owner * 16, 16), 16)

    half_columns = (pl.ds(0, D // 2), pl.ds(D // 2, D // 2))
    relayed, weighed, summed = receiver(), receiver(), receiver()
    for i, distance in enumerate((1, -1)):
        send(w_out.at[y_rows(4), half_columns[i]], relay.at[i], y_device(distance), relayed)
    for src, dst in weight_moves:
        send(src, dst, sibling, weighed, 1)
    for i, distance in enumerate((1, -1, 2, -2)):
        send(w_out.at[y_rows(distance), :], y_in.at[i], y_device(distance), summed)

    local[3].wait()
    row_at = lax.broadcasted_iota(jnp.int32, (SEQ, SEQ), 0)
    column_at = lax.broadcasted_iota(jnp.int32, (SEQ, SEQ), 1)
    documents = jnp.broadcast_to(docs[...].astype(F32), (SEQ, SEQ))
    own_document = jnp.sum(
        jnp.where(row_at == column_at, documents, 0.0), axis=-1, keepdims=True
    )
    allowed = (column_at <= row_at) & (documents == own_document)
    bias[...] = jnp.where(allowed, 0.0, -1e30)

    def from_side(i):
        return (3, 1)[i]

    for k in chunks:
        wait_bytes_of(normed_all.at[z, pl.ds(0, 2), :, columns(k)], normed_near[k])
        part = normed_part(z, x_at[from_side(k % 2)], k)
        send(part, part, sides[k % 2], normed_far[k])
        if k != z_first:
            for i in range(2):
                part = normed_part(z, x_at[from_side(i)], k)
                send(part, part, across, normed_crossed[k])
        wait_bytes_of(grads_part(other_z, x, k), grads_crossed[k])
        part = grads_all.at[:, x, :, columns(k)]
        for side in sides:
            send(part, part, side, grads_near[k])

    for copy in local[4 : N_LOCAL - 1]:
        copy.wait()
    all_weights = w_in.at[pl.ds(0, 3456), :]
    wait_bytes_of(all_weights, local_sems.at[N_LOCAL - 1])
    wait_bytes_of(all_weights, weighed)
    wait_bytes_of(relay, relayed)
    for i, distance in enumerate((3, -3)):
        far[i] = w_back[y_rows(distance, c * HEAD_DIM), :]
        far[i, :, half_columns[i]] = (
            far[i, :, half_columns[i]].astype(F32) + relay[i].astype(F32)
        ).astype(BF16)
        send(far.at[i], y_in.at[4 + i], y_device(distance), summed)

    wait_bytes_of(normed_part(other_z, x, z_first), normed_crossed[z_first])
    part = normed_part(other_z, x, z_first)
    crossed_near, crossed_far = receiver(), receiver()
    for side in sides:
        send(part, part, side, crossed_near)
    for k in chunks:
        wait_bytes_of(normed_part(z, x_at[2], k), normed_far[k])
        if k != z_first:
            part = normed_part(z, x_at[2], k)
            send(part, part, across, normed_crossed[k])
    for k in chunks:
        wait_bytes_of(grads_all.at[:, pl.ds(0, 2), :, columns(k)], grads_near[k])
        part = grads_all.at[:, x_at[from_side(k % 2)], :, columns(k)]
        send(part, part, sides[k % 2], grads_far[k])
        if k == 1:
            wait_bytes_of(normed_all.at[z, pl.ds(0, 2), :, columns(z_first)], crossed_near)
            part = normed_part(other_z, x_at[from_side(z_first % 2)], z_first)
            send(part, part, sides[z_first % 2], crossed_far)

    acc_back[...] = jnp.zeros_like(acc_back)
    acc_in[...] = jnp.zeros_like(acc_in)
    for k in chunks:
        wait_bytes_of(grads_all.at[:, x_at[2], :, columns(k)], grads_far[k])
        acc_back[...] += lax.dot_general(
            grads_all[:, :, :, columns(k)].reshape(HALF, GW), w_back[:, columns(k)],
            CONTRACT_LAST, preferred_element_type=F32,
        )
    wait_bytes_of(y_in, summed)
    total = w_back[y_rows(0, c * HEAD_DIM), :].astype(F32)
    for i in range(6):
        total = total + y_in[i].astype(F32)
    totals[...] = total
    for i in range(Z_HI):
        z_out[i] = totals[i * OUTER_ROWS : (i + 1) * OUTER_ROWS, :].astype(BF16)
    line = {}

    upward, downward = receiver(), receiver()

    def line_copy(name, src, dst, step):
        line[name] = pltpu.make_async_remote_copy(
            src_ref=src, dst_ref=dst, send_sem=send_sems.at[2 if step > 0 else 3],
            recv_sem=upward if step > 0 else downward,
            device_id=z_device(step), device_id_type=MESH,
        )

    line_copy("up0", z_out.at[pl.ds(1, 3)], up_in, 1)
    line_copy("up1", up_out.at[pl.ds(0, 2)], up_in.at[pl.ds(1, 2)], 1)
    line_copy("up2", up_out.at[pl.ds(2, 1)], up_in.at[pl.ds(2, 1)], 1)
    line_copy("down3", z_out.at[pl.ds(0, 3)], down_in, -1)
    line_copy("down2", down_out.at[pl.ds(0, 2)], down_in.at[pl.ds(0, 2)], -1)
    line_copy("down1", down_out.at[pl.ds(2, 1)], down_in.at[pl.ds(0, 1)], -1)

    def at(position):
        return pl.when(zh == position)

    def line_sum(first, second):
        return (first.astype(F32) + second.astype(F32)).astype(BF16)

    @at(0)
    def _():
        line["up0"].start()

    @at(3)
    def _():
        line["down3"].start()

    for k in chunks:
        if k == z_first:
            wait_bytes_of(normed_part(other_z, x_at[2], k), crossed_far)
        else:
            wait_bytes_of(normed_all.at[other_z, :, :, columns(k)], normed_crossed[k])
        acc_in[...] += jnp.dot(
            normed_all[:, :, :, columns(k)].reshape(HALF, GW), w_in[columns(k), :],
            preferred_element_type=F32,
        )

    def blocks(value):
        return value.reshape(8, ROWS, HEAD_DIM)

    first = c == 0

    def column_block(ref, i):
        return ref[:, i * HEAD_DIM : (i + 1) * HEAD_DIM]

    queries = [blocks(column_block(acc_in, i) * width_scale).astype(BF16) for i in range(2)]
    head_grads = [blocks(column_block(acc_back, i) * out_scale).astype(BF16) for i in range(2)]
    keyval = [blocks(column_block(acc_in, i) * width_scale).astype(BF16) for i in (2, 3)]

    def pick(pair, condition):
        return jnp.where(condition, pair[0].astype(F32), pair[1].astype(F32)).astype(BF16)

    heads_out[0] = pick(queries, ~first)
    heads_out[1] = pick(head_grads, ~first)
    heads_out[2] = keyval[0]
    heads_out[3] = keyval[1]
    exchanged, returned = receiver(), receiver()
    send(heads_out, heads.at[:, :, c], sibling, exchanged)
    heads[0, :, c] = pick(queries, first)
    heads[1, :, c] = pick(head_grads, first)
    heads[2, :, c] = keyval[0]
    heads[3, :, c] = keyval[1]
    wait_bytes_of(heads_out, exchanged)

    def sequence(i):
        return heads[i].astype(F32).reshape(SEQ, HEAD_DIM).astype(BF16)

    query, head_grad, key, value = [sequence(i) for i in range(4)]
    key_parts, value_parts = [None] * 3, [None] * 3
    for i in range(3):
        limit = (i + 1) * 128
        here = slice(i * 128, limit)
        scores = lax.dot_general(
            query[here], key[:limit], CONTRACT_LAST, preferred_element_type=F32
        )
        scores = scores * score_scale + bias[here, :limit]
        powers = jnp.exp(scores - jnp.max(scores, axis=-1, keepdims=True))
        probs = powers / jnp.sum(powers, axis=-1, keepdims=True)
        prob_grads = lax.dot_general(
            head_grad[here], value[:limit], CONTRACT_LAST, preferred_element_type=F32
        )
        score_grads = (
            probs
            * (prob_grads - jnp.sum(probs * prob_grads, axis=-1, keepdims=True))
            * score_scale
        ).astype(BF16)
        probs_low = probs.astype(BF16)
        query_grads = jnp.dot(score_grads, key[:limit], preferred_element_type=F32)
        grad_rows[0, here] = query_grads
        for j in range(i + 1):
            there = slice(j * 128, (j + 1) * 128)
            key_term = lax.dot_general(
                score_grads[:, there], query[here], CONTRACT_FIRST, preferred_element_type=F32
            )
            value_term = lax.dot_general(
                probs_low[:, there], head_grad[here], CONTRACT_FIRST, preferred_element_type=F32
            )
            key_parts[j] = key_term if i == j else key_parts[j] + key_term
            value_parts[j] = value_term if i == j else value_parts[j] + value_term
    for j in range(3):
        there = slice(j * 128, (j + 1) * 128)
        grad_rows[1, there] = key_parts[j]
        grad_rows[2, there] = value_parts[j]
    for i in range(3):
        back[i] = grad_rows[i].reshape(8, 2, ROWS, HEAD_DIM).astype(BF16)
    send(back.at[:, :, other_c], back_in, sibling, returned)

    @at(1)
    def _():
        line["up0"].wait_recv()
        up_out[0:2] = line_sum(z_out[2:4], up_in[1:3])
        line["up1"].start()

    @at(2)
    def _():
        line["down3"].wait_recv()
        down_out[0:2] = line_sum(z_out[0:2], down_in[0:2])
        line["down2"].start()

    wait_bytes_of(back_in, returned)

    def own_rows(i):
        return back[i, :, c].astype(F32).reshape(HALF, HEAD_DIM)

    def received_rows(i):
        return back_in[i].astype(F32).reshape(HALF, HEAD_DIM)

    query_pair = (own_rows(0), received_rows(0))
    upstream = jnp.concatenate(
        [
            jnp.where(first, query_pair[0], query_pair[1]).astype(BF16),
            jnp.where(first, query_pair[1], query_pair[0]).astype(BF16),
            (own_rows(1) + received_rows(1)).astype(BF16),
            (own_rows(2) + received_rows(2)).astype(BF16),
        ],
        axis=1,
    )

    def sum_columns(j):
        return pl.ds(j * SW, SW)

    hopped, neared, crossed = [[receiver() for _ in range(SUMS)] for _ in range(3)]
    plan = list(enumerate(SUM_PLAN))
    by_x = [(j, way) for j, (kind, way) in plan if kind == "x"]
    by_z = [(j, way) for j, (kind, way) in plan if kind == "z"]
    slot_of = {j: slot for group in (by_x, by_z) for slot, (j, _) in enumerate(group)}
    forward_slot = {0: 1, 1: 3}
    for j, (kind, way) in plan:
        term = lax.dot_general(
            upstream, w_in[sum_columns(j), :], CONTRACT_LAST, preferred_element_type=F32
        )
        terms[:, :, :, sum_columns(j)] = (
            (term * width_scale).reshape(2, 4, ROWS, SW).astype(BF16)
        )
        slot = slot_of[j]
        if kind == "z":
            part = terms.at[other_z, :, :, sum_columns(j)]
            send(part, from_z_z.at[slot], across, crossed[j], 4)
        else:
            part = terms.at[:, x_at[2], :, sum_columns(j)]
            send(part, hop_x.at[slot], sides[way], hopped[j], 5)
            part = terms.at[:, x_at[forward_slot[1 - way]], :, sum_columns(j)]
            send(part, near_x.at[slot, 0], sides[1 - way], neared[j], 5)

    for slot, (j, way) in enumerate(by_x):
        forward = forward_slot[way]
        wait_bytes_of(hop_x.at[slot], hopped[j])
        terms[:, x_at[forward], :, sum_columns(j)] = (
            terms[:, x_at[forward], :, sum_columns(j)].astype(F32) + hop_x[slot].astype(F32)
        ).astype(BF16)
        part = terms.at[:, x_at[forward], :, sum_columns(j)]
        send(part, near_x.at[slot, 1], sides[way], neared[j], 5)
    for slot, (j, way) in enumerate(by_z):
        wait_bytes_of(from_z_z.at[slot], crossed[j])
        terms[z, :, :, sum_columns(j)] = (
            terms[z, :, :, sum_columns(j)].astype(F32) + from_z_z[slot].astype(F32)
        ).astype(BF16)
        part = terms.at[z, x_at[2], :, sum_columns(j)]
        send(part, hop_z.at[slot], sides[way], hopped[j], 4)
        part = terms.at[z, x_at[forward_slot[1 - way]], :, sum_columns(j)]
        send(part, near_z.at[slot, 0], sides[1 - way], neared[j], 4)

    @at(2)
    def _():
        line["up1"].wait_recv()
        up_out[2:3] = line_sum(z_out[3:4], up_in[2:3])
        line["up2"].start()

    @at(1)
    def _():
        line["down2"].wait_recv()
        down_out[2:3] = line_sum(z_out[0:1], down_in[0:1])
        line["down1"].start()

    for slot, (j, way) in enumerate(by_x):
        wait_bytes_of(near_x.at[slot], neared[j])
        terms[:, x, :, sum_columns(j)] = (
            terms[:, x, :, sum_columns(j)].astype(F32)
            + near_x[slot, 0].astype(F32)
            + near_x[slot, 1].astype(F32)
        ).astype(BF16)
        part = terms.at[other_z, x, :, sum_columns(j)]
        send(part, from_z_x.at[slot], across, crossed[j], 6)
    for slot, (j, way) in enumerate(by_z):
        forward = forward_slot[way]
        wait_bytes_of(hop_z.at[slot], hopped[j])
        terms[z, x_at[forward], :, sum_columns(j)] = (
            terms[z, x_at[forward], :, sum_columns(j)].astype(F32) + hop_z[slot].astype(F32)
        ).astype(BF16)
        part = terms.at[z, x_at[forward], :, sum_columns(j)]
        send(part, near_z.at[slot, 1], sides[way], neared[j], 4)

    @at(0)
    def _():
        line["down1"].wait_recv()
        mine[...] = z_out[0].astype(F32) + down_in[0].astype(F32)

    @at(1)
    def _():
        mine[...] = z_out[1].astype(F32) + up_in[0].astype(F32) + down_in[1].astype(F32)

    @at(2)
    def _():
        mine[...] = z_out[2].astype(F32) + up_in[1].astype(F32) + down_in[2].astype(F32)

    @at(3)
    def _():
        line["up2"].wait_recv()
        mine[...] = z_out[3].astype(F32) + up_in[2].astype(F32)

    mean = mine[...]
    mean = mean * (1.0 / N_REPLICA)
    delta = outer_params[...] - mean
    moment = 0.9 * outer_moment[...] + delta
    new_moment[...] = moment
    new_params[...] = outer_params[...] - 0.7 * (delta + 0.9 * moment)

    normed_grads = [None] * SUMS
    for slot, (j, way) in enumerate(by_x):
        wait_bytes_of(from_z_x.at[slot], crossed[j])
        normed_grads[j] = terms[z, x, :, sum_columns(j)].astype(F32) + from_z_x[slot].astype(F32)
    for slot, (j, way) in enumerate(by_z):
        wait_bytes_of(near_z.at[slot], neared[j])
        normed_grads[j] = (
            terms[z, x, :, sum_columns(j)].astype(F32)
            + near_z[slot, 0].astype(F32)
            + near_z[slot, 1].astype(F32)
        )
    scaled = jnp.concatenate(normed_grads, axis=1) * gain[...]
    centered = inputs[...].astype(F32) * inv_rms
    projected = jnp.sum(scaled * centered, axis=-1, keepdims=True) * (1.0 / D)
    input_grads[...] = (
        out_grads[...].astype(F32) + inv_rms * (scaled - centered * projected)
    ).astype(BF16)
    assert next(receivers, None) is None
    wait_bytes_of(w_in.at[pl.ds(0, 4368), :], send_sems.at[0])
    wait_bytes_of(all_weights, send_sems.at[1])
    wait_bytes_of(terms.at[0, :, :, pl.ds(0, 7 * SW)], send_sems.at[4])
    wait_bytes_of(terms.at[:, pl.ds(0, 3), :, pl.ds(0, 5 * SW)], send_sems.at[5])
    wait_bytes_of(terms.at[0, 0, :, pl.ds(0, 5 * SW)], send_sems.at[6])
    for position, names in enumerate((("up0",), ("up1", "down1"), ("up2", "down2"), ("down3",))):

        @at(position)
        def _():
            for name in names:
                line[name].wait_send()


def write_out(first, second, third, first_out, second_out, third_out, *scratch):
    held, (in_sems, out_sems) = scratch[:3], scratch[3:]
    results = (first_out, second_out, third_out)
    loads = [
        pltpu.make_async_copy(src, held[i], in_sems.at[i])
        for i, src in enumerate((first, second, third))
    ]
    stores = [
        pltpu.make_async_copy(held[i], dst.at[0], out_sems.at[i]) for i, dst in enumerate(results)
    ]
    for load in loads:
        load.start()
    for load, store in zip(loads, stores):
        load.wait()
        store.start()
    for store in stores:
        store.wait()


def on_device(
    inputs, out_grads, norm_gain, doc_ids, w_query, w_keyval, w_out, outer_params, outer_moment
):
    vmem = pl.BlockSpec(memory_space=pltpu.VMEM)
    hbm = pl.BlockSpec(memory_space=pltpu.HBM)
    anywhere = pl.BlockSpec(memory_space=pl.ANY)
    by_x = sum(kind == "x" for kind, _ in SUM_PLAN)
    by_z = SUMS - by_x
    input_grads, new_params, new_moment = pl.pallas_call(
        kernel,
        out_shape=(
            jax.ShapeDtypeStruct((ROWS, D), BF16),
            jax.ShapeDtypeStruct((OUTER_ROWS, D), F32),
            jax.ShapeDtypeStruct((OUTER_ROWS, D), F32),
        ),
        in_specs=[hbm] * 9,
        out_specs=(vmem, vmem, vmem),
        scratch_shapes=[
            pltpu.VMEM((ROWS, D), BF16),
            pltpu.VMEM((ROWS, D), BF16),
            pltpu.VMEM((1, D), F32),
            pltpu.VMEM((1, SEQ), jnp.int32),
            pltpu.VMEM((OUTER_ROWS, D), F32),
            pltpu.VMEM((OUTER_ROWS, D), F32),
            pltpu.VMEM((2, 4, ROWS, D), BF16),
            pltpu.VMEM((2, 4, ROWS, D), BF16),
            pltpu.VMEM((D, 4 * HEAD_DIM), BF16),
            pltpu.VMEM((2 * HEAD_DIM, D), BF16),
            pltpu.VMEM((SEQ, SEQ), F32),
            pltpu.VMEM((HALF, 4 * HEAD_DIM), F32),
            pltpu.VMEM((HALF, 2 * HEAD_DIM), F32),
            pltpu.VMEM((4, 8, 2, ROWS, HEAD_DIM), BF16),
            pltpu.VMEM((4, 8, ROWS, HEAD_DIM), BF16),
            pltpu.VMEM((3, 8, 2, ROWS, HEAD_DIM), BF16),
            pltpu.VMEM((3, 8, ROWS, HEAD_DIM), BF16),
            pltpu.VMEM((3, 8, ROWS, HEAD_DIM), BF16),
            pltpu.VMEM((3, SEQ, HEAD_DIM), F32),
            pltpu.VMEM((2, 4, ROWS, D), BF16),
            pltpu.VMEM((by_x, 2, ROWS, SW), BF16),
            pltpu.VMEM((by_x, 2, 2, ROWS, SW), BF16),
            pltpu.VMEM((by_z, ROWS, SW), BF16),
            pltpu.VMEM((by_z, 2, ROWS, SW), BF16),
            pltpu.VMEM((by_x, ROWS, SW), BF16),
            pltpu.VMEM((by_z, 4, ROWS, SW), BF16),
            pltpu.VMEM((16, D), F32),
            pltpu.VMEM((2, 16, D // 2), BF16),
            pltpu.VMEM((2, 16, D), BF16),
            pltpu.VMEM((6, 16, D), BF16),
            pltpu.VMEM((Z_HI, OUTER_ROWS, D), BF16),
            pltpu.VMEM((Z_HI - 1, OUTER_ROWS, D), BF16),
            pltpu.VMEM((Z_HI - 1, OUTER_ROWS, D), BF16),
            pltpu.VMEM((Z_HI - 1, OUTER_ROWS, D), BF16),
            pltpu.VMEM((Z_HI - 1, OUTER_ROWS, D), BF16),
            pltpu.VMEM((OUTER_ROWS, D), F32),
            pltpu.SemaphoreType.DMA((N_SEND,)),
            pltpu.SemaphoreType.DMA((N_RECEIVE,)),
            pltpu.SemaphoreType.DMA((N_LOCAL,)),
        ],
        compiler_params=pltpu.CompilerParams(
            collective_id=0, has_side_effects=True, vmem_limit_bytes=63 * 2**20
        ),
        name="layer_backward",
    )(
        inputs[0], out_grads[0], norm_gain, doc_ids, w_query[0], w_keyval[0], w_out[0],
        outer_params[0], outer_moment[0],
    )
    input_grads, new_params, new_moment = pl.pallas_call(
        write_out,
        out_shape=(
            jax.ShapeDtypeStruct((1, ROWS, D), BF16),
            jax.ShapeDtypeStruct((1, OUTER_ROWS, D), F32),
            jax.ShapeDtypeStruct((1, OUTER_ROWS, D), F32),
        ),
        in_specs=[anywhere] * 3,
        out_specs=[anywhere] * 3,
        scratch_shapes=[
            pltpu.VMEM((ROWS, D), BF16),
            pltpu.VMEM((OUTER_ROWS, D), F32),
            pltpu.VMEM((OUTER_ROWS, D), F32),
            pltpu.SemaphoreType.DMA((3,)),
            pltpu.SemaphoreType.DMA((3,)),
        ],
        compiler_params=pltpu.CompilerParams(vmem_limit_bytes=63 * 2**20),
        name="write_out",
    )(input_grads, new_params, new_moment)
    return input_grads, new_params, new_moment


def solution(mesh):
    placed = (
        P("replica", "mp", None),
        P("replica", "mp", None),
        P(),
        P("replica", None),
        P("replica", None, "mp"),
        P("replica", None, "mp"),
        P("replica", "mp", None),
        P("mp", "replica", None),
        P("mp", "replica", None),
    )
    return jax.shard_map(
        on_device,
        mesh=mesh,
        in_specs=placed,
        out_specs=(P("replica", "mp", None), P("mp", "replica", None), P("mp", "replica", None)),
        check_vma=False,
    )
```

```python
import jax
import jax.numpy as jnp
from jax import lax
from jax.experimental import pallas as pl
from jax.experimental.pallas import tpu as pltpu
from jax.sharding import PartitionSpec as P

D = 4608
HEAD_DIM = 128
SEQ = 384
ROWS = 24
HALF = 192
GATHER = 6
GW = D // GATHER
SUMS = 12
SW = D // SUMS
Y_SIZE = 8
Z_HI = 4
OUTER_ROWS = 4
N_REPLICA = 32
MESH = pl.DeviceIdType.MESH
F32 = jnp.float32
BF16 = jnp.bfloat16
CONTRACT_LAST = (((1,), (1,)), ((), ()))
CONTRACT_FIRST = (((0,), (0,)), ((), ()))
N_RECEIVE = 82
N_SEND = 8
N_LOCAL = 8
SUM_PLAN = (
    ("z", 1), ("x", 0), ("z", 0), ("x", 1), ("z", 1), ("x", 0), ("x", 1), ("z", 0), ("x", 0), ("x", 1), ("x", 0), ("x", 1),
)


def kernel(
    inputs_hbm, out_grads_hbm, gain_hbm, docs_hbm, w_query, w_keyval, w_out, params_hbm, moment_hbm,
    input_grads, new_params, new_moment,
    inputs, out_grads, gain, docs, outer_params, outer_moment,
    normed_all, grads_all, w_in, w_back, bias, acc_in, acc_back, heads, heads_out,
    back, back_out, back_in, grad_rows, terms, hop_x, near_x, hop_z, near_z, from_z_x, from_z_z,
    totals, relay, far, y_in, z_out, up_in, up_out, down_in, down_out, mine,
    send_sems, recv_sems, local_sems, meet,
):
    width_scale = D ** (-0.5)
    score_scale = 144.0 ** (-0.5)
    out_scale = (16 * HEAD_DIM) ** (-0.5)
    replica = lax.axis_index("replica")
    model = lax.axis_index("mp")
    c = lax.rem(model, 2)
    x = lax.rem(lax.div(model, 2), 4)
    z = lax.div(model, 8)
    y = lax.div(replica, Z_HI)
    zh = lax.rem(replica, Z_HI)
    other_c = 1 - c
    other_z = 1 - z
    x_at = [lax.rem(x + i, 4) for i in range(4)]

    def on_model(zz, xx, cc):
        return (replica, (zz * 4 + xx) * 2 + cc)

    right = on_model(z, x_at[1], c)
    left = on_model(z, x_at[3], c)
    across = on_model(other_z, x, c)
    sibling = on_model(z, x, other_c)
    sides = (right, left)

    def y_device(distance):
        return (lax.rem(y + distance + Y_SIZE, Y_SIZE) * Z_HI + zh, model)

    def z_device(distance):
        return (replica + distance, model)

    partners = [right, left, across, sibling]
    partners += [y_device(d) for d in (1, -1)]
    outward = 2 * z - 1
    has_outward = jnp.where(z == 1, zh < Z_HI - 1, zh > 0)
    outward_device = (replica + outward, (other_z * 4 + x) * 2 + c)

    def signal(semaphore, device):
        pl.semaphore_signal(semaphore, inc=1, device_id=device, device_id_type=MESH)

    barrier = pltpu.get_barrier_semaphore()
    for partner in partners:
        signal(barrier, partner)

    @pl.when(has_outward)
    def _():
        signal(barrier, outward_device)

    own_columns = pl.ds(pl.multiple_of(c * HEAD_DIM, HEAD_DIM), HEAD_DIM)
    own_keyval = pl.ds(pl.multiple_of(2 * HEAD_DIM + c * HEAD_DIM, HEAD_DIM), HEAD_DIM)
    weight_moves = (
        (w_out, w_back.at[own_columns, :]),
        (w_query, w_in.at[:, own_columns]),
        (w_keyval, w_in.at[:, own_keyval]),
    )
    moves = (
        (inputs_hbm, inputs),
        (gain_hbm, gain.at[0]),
        (out_grads_hbm, grads_all.at[z, x]),
        (docs_hbm, docs),
        (out_grads_hbm, out_grads),
        (params_hbm, outer_params),
        (moment_hbm, outer_moment),
    ) + weight_moves
    local = []
    for index, (src, dst) in enumerate(moves):
        copy = pltpu.make_async_copy(src, dst, local_sems.at[min(index, N_LOCAL - 1)])
        copy.start()
        local.append(copy)

    receivers = iter(range(N_RECEIVE))

    def receiver():
        return recv_sems.at[next(receivers)]

    def send(src, dst, device, arrival, group=0):
        copy = pltpu.make_async_remote_copy(
            src_ref=src, dst_ref=dst, send_sem=send_sems.at[group], recv_sem=arrival,
            device_id=device, device_id_type=MESH,
        )
        copy.start()

    def wait_bytes_of(ref, semaphore):
        pltpu.make_async_copy(ref, ref, semaphore).wait()

    local[0].wait()
    rows = inputs[...].astype(F32)
    inv_rms = lax.rsqrt(jnp.sum(rows * rows, axis=-1, keepdims=True) * (1.0 / D) + 1e-06)
    local[1].wait()
    normed_all[z, x] = (rows * inv_rms * gain[...]).astype(BF16)
    local[2].wait()

    @pl.when(has_outward)
    def _():
        pl.semaphore_wait(barrier, len(partners) + 1)

    @pl.when(~has_outward)
    def _():
        pl.semaphore_wait(barrier, len(partners))

    def columns(k):
        return pl.ds(k * GW, GW)

    def normed_part(zz, xx, k):
        return normed_all.at[zz, xx, :, columns(k)]

    def grads_part(zz, xx, k):
        return grads_all.at[zz, xx, :, columns(k)]

    chunks = range(GATHER)
    z_first = GATHER - 1
    normed_crossed, normed_near, normed_far = [[receiver() for _ in chunks] for _ in range(3)]
    grads_near, grads_far, grads_crossed = [[receiver() for _ in chunks] for _ in range(3)]
    for k in chunks:
        part = normed_part(z, x, k)
        send(part, part, across, normed_crossed[k])
        part = grads_part(z, x, k)
        for side in sides:
            send(part, part, side, grads_near[k])
    for k in chunks:
        part = grads_part(z, x, k)
        send(part, part, across, grads_crossed[k])

    y_far = {2: meet.at[0], -2: meet.at[1], 3: meet.at[2], -3: meet.at[3]}
    line_up, line_down = meet.at[4], meet.at[5]
    signal(y_far[2], y_device(-1))
    signal(y_far[-2], y_device(1))

    @pl.when((z == 1) & has_outward)
    def _():
        signal(line_up, across)
        signal(line_down, outward_device)

    @pl.when((z == 0) & has_outward)
    def _():
        signal(line_down, across)
        signal(line_up, outward_device)

    def y_rows(distance, base=0):
        owner = lax.rem(y + distance + Y_SIZE, Y_SIZE)
        return pl.ds(pl.multiple_of(base + owner * 16, 16), 16)

    half_columns = (pl.ds(0, D // 2), pl.ds(D // 2, D // 2))
    relayed, weighed, summed = receiver(), receiver(), receiver()
    for i, distance in enumerate((1, -1)):
        send(w_out.at[y_rows(4), half_columns[i]], relay.at[i], y_device(distance), relayed)
    for src, dst in weight_moves:
        send(src, dst, sibling, weighed, 1)
    for i, distance in enumerate((1, -1)):
        send(w_out.at[y_rows(distance), :], y_in.at[i], y_device(distance), summed)

    local[3].wait()
    row_at = lax.broadcasted_iota(jnp.int32, (SEQ, SEQ), 0)
    column_at = lax.broadcasted_iota(jnp.int32, (SEQ, SEQ), 1)
    documents = jnp.broadcast_to(docs[...].astype(F32), (SEQ, SEQ))
    own_document = jnp.sum(
        jnp.where(row_at == column_at, documents, 0.0), axis=-1, keepdims=True
    )
    allowed = (column_at <= row_at) & (documents == own_document)
    bias[...] = jnp.where(allowed, 0.0, -1e30)

    for i, distance in enumerate((2, -2)):
        pl.semaphore_wait(y_far[distance], 1)
        send(w_out.at[y_rows(distance), :], y_in.at[2 + i], y_device(distance), summed)
    signal(y_far[3], y_device(-1))
    signal(y_far[-3], y_device(2))

    def from_side(i):
        return (3, 1)[i]

    for k in chunks:
        wait_bytes_of(grads_all.at[z, pl.ds(0, 2), :, columns(k)], grads_near[k])
        part = grads_part(z, x_at[from_side(k % 2)], k)
        send(part, part, sides[k % 2], grads_far[k])
        if k != z_first:
            for i in range(2):
                part = grads_part(z, x_at[from_side(i)], k)
                send(part, part, across, grads_crossed[k])
        wait_bytes_of(normed_part(other_z, x, k), normed_crossed[k])
        part = normed_all.at[:, x, :, columns(k)]
        for side in sides:
            send(part, part, side, normed_near[k])

    for copy in local[4 : N_LOCAL - 1]:
        copy.wait()
    all_weights = w_in.at[pl.ds(0, 3456), :]
    wait_bytes_of(all_weights, local_sems.at[N_LOCAL - 1])
    wait_bytes_of(all_weights, weighed)
    wait_bytes_of(relay, relayed)
    for i, distance in enumerate((3, -3)):
        far[i] = w_back[y_rows(distance, c * HEAD_DIM), :]
        far[i, :, half_columns[i]] = (
            far[i, :, half_columns[i]].astype(F32) + relay[i].astype(F32)
        ).astype(BF16)
        pl.semaphore_wait(y_far[distance], 1)
        send(far.at[i], y_in.at[4 + i], y_device(distance), summed)

    wait_bytes_of(grads_part(other_z, x, z_first), grads_crossed[z_first])
    part = grads_part(other_z, x, z_first)
    crossed_near, crossed_far = receiver(), receiver()
    for side in sides:
        send(part, part, side, crossed_near)
    for k in chunks:
        wait_bytes_of(grads_part(z, x_at[2], k), grads_far[k])
        if k != z_first:
            part = grads_part(z, x_at[2], k)
            send(part, part, across, grads_crossed[k])
    for k in chunks:
        wait_bytes_of(normed_all.at[:, pl.ds(0, 2), :, columns(k)], normed_near[k])
        part = normed_all.at[:, x_at[from_side(k % 2)], :, columns(k)]
        send(part, part, sides[k % 2], normed_far[k])
        if k == 1:
            wait_bytes_of(grads_all.at[z, pl.ds(0, 2), :, columns(z_first)], crossed_near)
            part = grads_part(other_z, x_at[from_side(z_first % 2)], z_first)
            send(part, part, sides[z_first % 2], crossed_far)

    first = c == 0
    exchanged, exchanged_grads, returned = receiver(), receiver(), receiver()

    def blocks(ref, i, scale):
        part = ref[:, i * HEAD_DIM : (i + 1) * HEAD_DIM] * scale
        return part.reshape(8, ROWS, HEAD_DIM).astype(BF16)

    def pick(pair, condition):
        return jnp.where(condition, pair[0].astype(F32), pair[1].astype(F32)).astype(BF16)

    def sequence(i):
        return heads[i].astype(F32).reshape(SEQ, HEAD_DIM).astype(BF16)

    acc_in[...] = jnp.zeros_like(acc_in)
    acc_back[...] = jnp.zeros_like(acc_back)
    for k in chunks:
        wait_bytes_of(normed_all.at[:, x_at[2], :, columns(k)], normed_far[k])
        acc_in[...] += jnp.dot(
            normed_all[:, :, :, columns(k)].reshape(HALF, GW), w_in[columns(k), :],
            preferred_element_type=F32,
        )
    queries = [blocks(acc_in, i, width_scale) for i in range(2)]
    heads_out[0] = pick(queries, ~first)
    heads_out[1] = blocks(acc_in, 2, width_scale)
    heads_out[2] = blocks(acc_in, 3, width_scale)
    send(heads_out.at[pl.ds(0, 3)], heads.at[pl.ds(0, 3), :, c], sibling, exchanged)
    heads[0, :, c] = pick(queries, first)
    heads[1, :, c] = heads_out[1]
    heads[2, :, c] = heads_out[2]

    wait_bytes_of(y_in, summed)
    total = w_back[y_rows(0, c * HEAD_DIM), :].astype(F32)
    for i in range(6):
        total = total + y_in[i].astype(F32)
    totals[...] = total
    for i in range(Z_HI):
        z_out[i] = totals[i * OUTER_ROWS : (i + 1) * OUTER_ROWS, :].astype(BF16)
    line = {}

    upward, downward = receiver(), receiver()

    def line_copy(name, src, dst, step):
        line[name] = pltpu.make_async_remote_copy(
            src_ref=src, dst_ref=dst, send_sem=send_sems.at[2 if step > 0 else 3],
            recv_sem=upward if step > 0 else downward,
            device_id=z_device(step), device_id_type=MESH,
        )

    line_copy("up0", z_out.at[pl.ds(1, 3)], up_in, 1)
    line_copy("up1", up_out.at[pl.ds(0, 2)], up_in.at[pl.ds(1, 2)], 1)
    line_copy("up2", up_out.at[pl.ds(2, 1)], up_in.at[pl.ds(2, 1)], 1)
    line_copy("down3", z_out.at[pl.ds(0, 3)], down_in, -1)
    line_copy("down2", down_out.at[pl.ds(0, 2)], down_in.at[pl.ds(0, 2)], -1)
    line_copy("down1", down_out.at[pl.ds(2, 1)], down_in.at[pl.ds(0, 1)], -1)

    def at(position):
        return pl.when(zh == position)

    def line_sum(first, second):
        return (first.astype(F32) + second.astype(F32)).astype(BF16)

    @pl.when(zh < Z_HI - 1)
    def _():
        pl.semaphore_wait(line_up, 1)

    @pl.when(zh > 0)
    def _():
        pl.semaphore_wait(line_down, 1)

    @at(0)
    def _():
        line["up0"].start()

    @at(3)
    def _():
        line["down3"].start()

    for k in chunks:
        if k == z_first:
            wait_bytes_of(grads_part(other_z, x_at[2], k), crossed_far)
        else:
            wait_bytes_of(grads_all.at[other_z, :, :, columns(k)], grads_crossed[k])
        acc_back[...] += lax.dot_general(
            grads_all[:, :, :, columns(k)].reshape(HALF, GW), w_back[:, columns(k)],
            CONTRACT_LAST, preferred_element_type=F32,
        )
    head_grads = [blocks(acc_back, i, out_scale) for i in range(2)]
    heads_out[3] = pick(head_grads, ~first)
    send(heads_out.at[3], heads.at[3, :, c], sibling, exchanged_grads)
    heads[3, :, c] = pick(head_grads, first)

    wait_bytes_of(heads_out.at[pl.ds(0, 3)], exchanged)
    query, key, value = [sequence(i) for i in range(3)]
    row_blocks = [(slice(i * 128, (i + 1) * 128), (i + 1) * 128) for i in range(3)]
    all_probs = []
    for here, limit in row_blocks:
        scores = lax.dot_general(
            query[here], key[:limit], CONTRACT_LAST, preferred_element_type=F32
        )
        scores = scores * score_scale + bias[here, :limit]
        powers = jnp.exp(scores - jnp.max(scores, axis=-1, keepdims=True))
        all_probs.append(powers / jnp.sum(powers, axis=-1, keepdims=True))

    wait_bytes_of(heads_out.at[3], exchanged_grads)
    head_grad = sequence(3)
    key_parts, value_parts = [None] * 3, [None] * 3
    for i, (here, limit) in enumerate(row_blocks):
        probs = all_probs[i]
        prob_grads = lax.dot_general(
            head_grad[here], value[:limit], CONTRACT_LAST, preferred_element_type=F32
        )
        score_grads = (
            probs
            * (prob_grads - jnp.sum(probs * prob_grads, axis=-1, keepdims=True))
            * score_scale
        ).astype(BF16)
        probs_low = probs.astype(BF16)
        grad_rows[0, here] = jnp.dot(
            score_grads, key[:limit], preferred_element_type=F32
        )
        for j in range(i + 1):
            there = slice(j * 128, (j + 1) * 128)
            key_term = lax.dot_general(
                score_grads[:, there], query[here], CONTRACT_FIRST, preferred_element_type=F32
            )
            value_term = lax.dot_general(
                probs_low[:, there], head_grad[here], CONTRACT_FIRST, preferred_element_type=F32
            )
            key_parts[j] = key_term if i == j else key_parts[j] + key_term
            value_parts[j] = value_term if i == j else value_parts[j] + value_term
    for j in range(3):
        there = slice(j * 128, (j + 1) * 128)
        grad_rows[1, there] = key_parts[j]
        grad_rows[2, there] = value_parts[j]
    for i in range(3):
        back[i] = grad_rows[i].reshape(8, 2, ROWS, HEAD_DIM).astype(BF16)
    send(back.at[:, :, other_c], back_in, sibling, returned)

    @at(1)
    def _():
        line["up0"].wait_recv()
        up_out[0:2] = line_sum(z_out[2:4], up_in[1:3])
        line["up1"].start()

    @at(2)
    def _():
        line["down3"].wait_recv()
        down_out[0:2] = line_sum(z_out[0:2], down_in[0:2])
        line["down2"].start()

    wait_bytes_of(back_in, returned)

    def own_rows(i):
        return back[i, :, c].astype(F32).reshape(HALF, HEAD_DIM)

    def received_rows(i):
        return back_in[i].astype(F32).reshape(HALF, HEAD_DIM)

    query_pair = (own_rows(0), received_rows(0))
    upstream = jnp.concatenate(
        [
            jnp.where(first, query_pair[0], query_pair[1]).astype(BF16),
            jnp.where(first, query_pair[1], query_pair[0]).astype(BF16),
            (own_rows(1) + received_rows(1)).astype(BF16),
            (own_rows(2) + received_rows(2)).astype(BF16),
        ],
        axis=1,
    )

    def sum_columns(j):
        return pl.ds(j * SW, SW)

    hopped, neared, crossed = [[receiver() for _ in range(SUMS)] for _ in range(3)]
    plan = list(enumerate(SUM_PLAN))
    by_x = [(j, way) for j, (kind, way) in plan if kind == "x"]
    by_z = [(j, way) for j, (kind, way) in plan if kind == "z"]
    slot_of = {j: slot for group in (by_x, by_z) for slot, (j, _) in enumerate(group)}
    forward_slot = {0: 1, 1: 3}
    for j, (kind, way) in plan:
        term = lax.dot_general(
            upstream, w_in[sum_columns(j), :], CONTRACT_LAST, preferred_element_type=F32
        )
        terms[:, :, :, sum_columns(j)] = (
            (term * width_scale).reshape(2, 4, ROWS, SW).astype(BF16)
        )
        slot = slot_of[j]
        if kind == "z":
            part = terms.at[other_z, :, :, sum_columns(j)]
            send(part, from_z_z.at[slot], across, crossed[j], 4)
        else:
            part = terms.at[:, x_at[2], :, sum_columns(j)]
            send(part, hop_x.at[slot], sides[way], hopped[j], 5)
            part = terms.at[:, x_at[forward_slot[1 - way]], :, sum_columns(j)]
            send(part, near_x.at[slot, 0], sides[1 - way], neared[j], 5)

    for slot, (j, way) in enumerate(by_x):
        forward = forward_slot[way]
        wait_bytes_of(hop_x.at[slot], hopped[j])
        terms[:, x_at[forward], :, sum_columns(j)] = (
            terms[:, x_at[forward], :, sum_columns(j)].astype(F32) + hop_x[slot].astype(F32)
        ).astype(BF16)
        part = terms.at[:, x_at[forward], :, sum_columns(j)]
        send(part, near_x.at[slot, 1], sides[way], neared[j], 5)
    for slot, (j, way) in enumerate(by_z):
        wait_bytes_of(from_z_z.at[slot], crossed[j])
        terms[z, :, :, sum_columns(j)] = (
            terms[z, :, :, sum_columns(j)].astype(F32) + from_z_z[slot].astype(F32)
        ).astype(BF16)
        part = terms.at[z, x_at[2], :, sum_columns(j)]
        send(part, hop_z.at[slot], sides[way], hopped[j], 7)
        part = terms.at[z, x_at[forward_slot[1 - way]], :, sum_columns(j)]
        send(part, near_z.at[slot, 0], sides[1 - way], neared[j], 7)

    @at(2)
    def _():
        line["up1"].wait_recv()
        up_out[2:3] = line_sum(z_out[3:4], up_in[2:3])
        line["up2"].start()

    @at(1)
    def _():
        line["down2"].wait_recv()
        down_out[2:3] = line_sum(z_out[0:1], down_in[0:1])
        line["down1"].start()

    for slot, (j, way) in enumerate(by_x):
        wait_bytes_of(near_x.at[slot], neared[j])
        terms[:, x, :, sum_columns(j)] = (
            terms[:, x, :, sum_columns(j)].astype(F32)
            + near_x[slot, 0].astype(F32)
            + near_x[slot, 1].astype(F32)
        ).astype(BF16)
        part = terms.at[other_z, x, :, sum_columns(j)]
        send(part, from_z_x.at[slot], across, crossed[j], 6)
    for slot, (j, way) in enumerate(by_z):
        forward = forward_slot[way]
        wait_bytes_of(hop_z.at[slot], hopped[j])
        terms[z, x_at[forward], :, sum_columns(j)] = (
            terms[z, x_at[forward], :, sum_columns(j)].astype(F32) + hop_z[slot].astype(F32)
        ).astype(BF16)
        part = terms.at[z, x_at[forward], :, sum_columns(j)]
        send(part, near_z.at[slot, 1], sides[way], neared[j], 7)

    @at(0)
    def _():
        line["down1"].wait_recv()
        mine[...] = z_out[0].astype(F32) + down_in[0].astype(F32)

    @at(1)
    def _():
        mine[...] = z_out[1].astype(F32) + up_in[0].astype(F32) + down_in[1].astype(F32)

    @at(2)
    def _():
        mine[...] = z_out[2].astype(F32) + up_in[1].astype(F32) + down_in[2].astype(F32)

    @at(3)
    def _():
        line["up2"].wait_recv()
        mine[...] = z_out[3].astype(F32) + up_in[2].astype(F32)

    mean = mine[...]
    mean = mean * (1.0 / N_REPLICA)
    delta = outer_params[...] - mean
    moment = 0.9 * outer_moment[...] + delta
    new_moment[...] = moment
    new_params[...] = outer_params[...] - 0.7 * (delta + 0.9 * moment)

    normed_grads = [None] * SUMS
    for slot, (j, way) in enumerate(by_x):
        wait_bytes_of(from_z_x.at[slot], crossed[j])
        normed_grads[j] = terms[z, x, :, sum_columns(j)].astype(F32) + from_z_x[slot].astype(F32)
    for slot, (j, way) in enumerate(by_z):
        wait_bytes_of(near_z.at[slot], neared[j])
        normed_grads[j] = (
            terms[z, x, :, sum_columns(j)].astype(F32)
            + near_z[slot, 0].astype(F32)
            + near_z[slot, 1].astype(F32)
        )
    scaled = jnp.concatenate(normed_grads, axis=1) * gain[...]
    centered = inputs[...].astype(F32) * inv_rms
    projected = jnp.sum(scaled * centered, axis=-1, keepdims=True) * (1.0 / D)
    input_grads[...] = (
        out_grads[...].astype(F32) + inv_rms * (scaled - centered * projected)
    ).astype(BF16)
    assert next(receivers, None) is None
    wait_bytes_of(w_in.at[pl.ds(0, 4368), :], send_sems.at[0])
    wait_bytes_of(all_weights, send_sems.at[1])
    x_columns, z_columns = pl.ds(0, len(by_x) * SW), pl.ds(0, len(by_z) * SW)
    wait_bytes_of(terms.at[0, :, :, z_columns], send_sems.at[4])
    wait_bytes_of(terms.at[:, pl.ds(0, 3), :, x_columns], send_sems.at[5])
    wait_bytes_of(terms.at[0, 0, :, x_columns], send_sems.at[6])
    wait_bytes_of(terms.at[0, pl.ds(0, 3), :, z_columns], send_sems.at[7])
    for position, names in enumerate((("up0",), ("up1", "down1"), ("up2", "down2"), ("down3",))):

        @at(position)
        def _():
            for name in names:
                line[name].wait_send()


def write_out(first, second, third, first_out, second_out, third_out, *scratch):
    held, (in_sems, out_sems) = scratch[:3], scratch[3:]
    results = (first_out, second_out, third_out)
    loads = [
        pltpu.make_async_copy(src, held[i], in_sems.at[i])
        for i, src in enumerate((first, second, third))
    ]
    stores = [
        pltpu.make_async_copy(held[i], dst.at[0], out_sems.at[i]) for i, dst in enumerate(results)
    ]
    for load in loads:
        load.start()
    for load, store in zip(loads, stores):
        load.wait()
        store.start()
    for store in stores:
        store.wait()


def on_device(
    inputs, out_grads, norm_gain, doc_ids, w_query, w_keyval, w_out, outer_params, outer_moment
):
    vmem = pl.BlockSpec(memory_space=pltpu.VMEM)
    hbm = pl.BlockSpec(memory_space=pltpu.HBM)
    anywhere = pl.BlockSpec(memory_space=pl.ANY)
    by_x = sum(kind == "x" for kind, _ in SUM_PLAN)
    by_z = SUMS - by_x
    input_grads, new_params, new_moment = pl.pallas_call(
        kernel,
        out_shape=(
            jax.ShapeDtypeStruct((ROWS, D), BF16),
            jax.ShapeDtypeStruct((OUTER_ROWS, D), F32),
            jax.ShapeDtypeStruct((OUTER_ROWS, D), F32),
        ),
        in_specs=[hbm] * 9,
        out_specs=(vmem, vmem, vmem),
        scratch_shapes=[
            pltpu.VMEM((ROWS, D), BF16),
            pltpu.VMEM((ROWS, D), BF16),
            pltpu.VMEM((1, D), F32),
            pltpu.VMEM((1, SEQ), jnp.int32),
            pltpu.VMEM((OUTER_ROWS, D), F32),
            pltpu.VMEM((OUTER_ROWS, D), F32),
            pltpu.VMEM((2, 4, ROWS, D), BF16),
            pltpu.VMEM((2, 4, ROWS, D), BF16),
            pltpu.VMEM((D, 4 * HEAD_DIM), BF16),
            pltpu.VMEM((2 * HEAD_DIM, D), BF16),
            pltpu.VMEM((SEQ, SEQ), F32),
            pltpu.VMEM((HALF, 4 * HEAD_DIM), F32),
            pltpu.VMEM((HALF, 2 * HEAD_DIM), F32),
            pltpu.VMEM((4, 8, 2, ROWS, HEAD_DIM), BF16),
            pltpu.VMEM((4, 8, ROWS, HEAD_DIM), BF16),
            pltpu.VMEM((3, 8, 2, ROWS, HEAD_DIM), BF16),
            pltpu.VMEM((3, 8, ROWS, HEAD_DIM), BF16),
            pltpu.VMEM((3, 8, ROWS, HEAD_DIM), BF16),
            pltpu.VMEM((3, SEQ, HEAD_DIM), F32),
            pltpu.VMEM((2, 4, ROWS, D), BF16),
            pltpu.VMEM((by_x, 2, ROWS, SW), BF16),
            pltpu.VMEM((by_x, 2, 2, ROWS, SW), BF16),
            pltpu.VMEM((by_z, ROWS, SW), BF16),
            pltpu.VMEM((by_z, 2, ROWS, SW), BF16),
            pltpu.VMEM((by_x, ROWS, SW), BF16),
            pltpu.VMEM((by_z, 4, ROWS, SW), BF16),
            pltpu.VMEM((16, D), F32),
            pltpu.VMEM((2, 16, D // 2), BF16),
            pltpu.VMEM((2, 16, D), BF16),
            pltpu.VMEM((6, 16, D), BF16),
            pltpu.VMEM((Z_HI, OUTER_ROWS, D), BF16),
            pltpu.VMEM((Z_HI - 1, OUTER_ROWS, D), BF16),
            pltpu.VMEM((Z_HI - 1, OUTER_ROWS, D), BF16),
            pltpu.VMEM((Z_HI - 1, OUTER_ROWS, D), BF16),
            pltpu.VMEM((Z_HI - 1, OUTER_ROWS, D), BF16),
            pltpu.VMEM((OUTER_ROWS, D), F32),
            pltpu.SemaphoreType.DMA((N_SEND,)),
            pltpu.SemaphoreType.DMA((N_RECEIVE,)),
            pltpu.SemaphoreType.DMA((N_LOCAL,)),
            pltpu.SemaphoreType.REGULAR((6,)),
        ],
        compiler_params=pltpu.CompilerParams(
            collective_id=0, has_side_effects=True, vmem_limit_bytes=63 * 2**20
        ),
        name="layer_backward",
    )(
        inputs[0], out_grads[0], norm_gain, doc_ids, w_query[0], w_keyval[0], w_out[0],
        outer_params[0], outer_moment[0],
    )
    input_grads, new_params, new_moment = pl.pallas_call(
        write_out,
        out_shape=(
            jax.ShapeDtypeStruct((1, ROWS, D), BF16),
            jax.ShapeDtypeStruct((1, OUTER_ROWS, D), F32),
            jax.ShapeDtypeStruct((1, OUTER_ROWS, D), F32),
        ),
        in_specs=[anywhere] * 3,
        out_specs=[anywhere] * 3,
        scratch_shapes=[
            pltpu.VMEM((ROWS, D), BF16),
            pltpu.VMEM((OUTER_ROWS, D), F32),
            pltpu.VMEM((OUTER_ROWS, D), F32),
            pltpu.SemaphoreType.DMA((3,)),
            pltpu.SemaphoreType.DMA((3,)),
        ],
        compiler_params=pltpu.CompilerParams(vmem_limit_bytes=63 * 2**20),
        name="write_out",
    )(input_grads, new_params, new_moment)
    return input_grads, new_params, new_moment


def solution(mesh):
    placed = (
        P("replica", "mp", None),
        P("replica", "mp", None),
        P(),
        P("replica", None),
        P("replica", None, "mp"),
        P("replica", None, "mp"),
        P("replica", "mp", None),
        P("mp", "replica", None),
        P("mp", "replica", None),
    )
    return jax.shard_map(
        on_device,
        mesh=mesh,
        in_specs=placed,
        out_specs=(P("replica", "mp", None), P("mp", "replica", None), P("mp", "replica", None)),
        check_vma=False,
    )
```

```python
import jax
import jax.numpy as jnp
from jax import lax
from jax.experimental import pallas as pl
from jax.experimental.pallas import tpu as pltpu
from jax.sharding import PartitionSpec as P

D = 4608
HEAD_DIM = 128
SEQ = 384
ROWS = 24
HALF = 192
GATHER = 6
GW = D // GATHER
SUMS = 12
SW = D // SUMS
Y_SIZE = 8
Z_HI = 4
OUTER_ROWS = 4
N_REPLICA = 32
MESH = pl.DeviceIdType.MESH
F32 = jnp.float32
BF16 = jnp.bfloat16
CONTRACT_LAST = (((1,), (1,)), ((), ()))
CONTRACT_FIRST = (((0,), (0,)), ((), ()))
N_RECEIVE = 82
N_SEND = 8
N_LOCAL = 8
SUM_PLAN = (
    ("z", 1), ("x", 0), ("z", 0), ("x", 1), ("z", 1), ("x", 0), ("x", 1), ("z", 0), ("x", 0), ("x", 1), ("x", 0), ("x", 1),
)
SUM_STEPS = (
    (1, 1), (1, 3), (1, 0), (1, 5), (1, 6), (1, 2), (1, 8), (1, 9), (1, 4), (1, 10), (1, 11), (1, 7), (2, 1), (2, 3), (2, 0), (2, 5), (2, 6), (2, 2), (2, 8), (2, 9), (2, 4), (2, 10), (2, 11), (2, 7),
)


def kernel(
    inputs_hbm, out_grads_hbm, gain_hbm, docs_hbm, w_query, w_keyval, w_out, params_hbm, moment_hbm,
    input_grads, new_params, new_moment,
    inputs, out_grads, gain, docs, outer_params, outer_moment,
    normed_all, grads_all, w_in, w_back, bias, acc_in, acc_back, heads, heads_out,
    back, back_out, back_in, grad_rows, terms, hop_x, near_x, hop_z, near_z, from_z_x, from_z_z,
    totals, relay, far, y_in, z_out, up_in, up_out, down_in, down_out, mine,
    send_sems, recv_sems, local_sems, meet,
):
    width_scale = D ** (-0.5)
    score_scale = 144.0 ** (-0.5)
    out_scale = (16 * HEAD_DIM) ** (-0.5)
    replica = lax.axis_index("replica")
    model = lax.axis_index("mp")
    c = lax.rem(model, 2)
    x = lax.rem(lax.div(model, 2), 4)
    z = lax.div(model, 8)
    y = lax.div(replica, Z_HI)
    zh = lax.rem(replica, Z_HI)
    other_c = 1 - c
    other_z = 1 - z
    x_at = [lax.rem(x + i, 4) for i in range(4)]

    def on_model(zz, xx, cc):
        return (replica, (zz * 4 + xx) * 2 + cc)

    right = on_model(z, x_at[1], c)
    left = on_model(z, x_at[3], c)
    across = on_model(other_z, x, c)
    sibling = on_model(z, x, other_c)
    sides = (right, left)

    def y_device(distance):
        return (lax.rem(y + distance + Y_SIZE, Y_SIZE) * Z_HI + zh, model)

    def z_device(distance):
        return (replica + distance, model)

    partners = [right, left, across, sibling]
    partners += [y_device(d) for d in (1, -1)]
    outward = 2 * z - 1
    has_outward = jnp.where(z == 1, zh < Z_HI - 1, zh > 0)
    outward_device = (replica + outward, (other_z * 4 + x) * 2 + c)

    def signal(semaphore, device):
        pl.semaphore_signal(semaphore, inc=1, device_id=device, device_id_type=MESH)

    barrier = pltpu.get_barrier_semaphore()
    for partner in partners:
        signal(barrier, partner)

    @pl.when(has_outward)
    def _():
        signal(barrier, outward_device)

    own_columns = pl.ds(pl.multiple_of(c * HEAD_DIM, HEAD_DIM), HEAD_DIM)
    own_keyval = pl.ds(pl.multiple_of(2 * HEAD_DIM + c * HEAD_DIM, HEAD_DIM), HEAD_DIM)
    weight_moves = (
        (w_out, w_back.at[own_columns, :]),
        (w_query, w_in.at[:, own_columns]),
        (w_keyval, w_in.at[:, own_keyval]),
    )
    moves = (
        (inputs_hbm, inputs),
        (gain_hbm, gain.at[0]),
        (out_grads_hbm, grads_all.at[z, x]),
        (docs_hbm, docs),
        (out_grads_hbm, out_grads),
        (params_hbm, outer_params),
        (moment_hbm, outer_moment),
    ) + weight_moves
    local = []
    for index, (src, dst) in enumerate(moves):
        copy = pltpu.make_async_copy(src, dst, local_sems.at[min(index, N_LOCAL - 1)])
        copy.start()
        local.append(copy)

    receivers = iter(range(N_RECEIVE))

    def receiver():
        return recv_sems.at[next(receivers)]

    def send(src, dst, device, arrival, group=0):
        copy = pltpu.make_async_remote_copy(
            src_ref=src, dst_ref=dst, send_sem=send_sems.at[group], recv_sem=arrival,
            device_id=device, device_id_type=MESH,
        )
        copy.start()

    def wait_bytes_of(ref, semaphore):
        pltpu.make_async_copy(ref, ref, semaphore).wait()

    local[0].wait()
    rows = inputs[...].astype(F32)
    inv_rms = lax.rsqrt(jnp.sum(rows * rows, axis=-1, keepdims=True) * (1.0 / D) + 1e-06)
    local[1].wait()
    normed_all[z, x] = (rows * inv_rms * gain[...]).astype(BF16)
    local[2].wait()

    @pl.when(has_outward)
    def _():
        pl.semaphore_wait(barrier, len(partners) + 1)

    @pl.when(~has_outward)
    def _():
        pl.semaphore_wait(barrier, len(partners))

    def columns(k):
        return pl.ds(k * GW, GW)

    def normed_part(zz, xx, k):
        return normed_all.at[zz, xx, :, columns(k)]

    def grads_part(zz, xx, k):
        return grads_all.at[zz, xx, :, columns(k)]

    chunks = range(GATHER)
    z_first = GATHER - 1
    normed_crossed, normed_near, normed_far = [[receiver() for _ in chunks] for _ in range(3)]
    grads_near, grads_far, grads_crossed = [[receiver() for _ in chunks] for _ in range(3)]
    for k in chunks:
        part = normed_part(z, x, k)
        send(part, part, across, normed_crossed[k])
        part = grads_part(z, x, k)
        for side in sides:
            send(part, part, side, grads_near[k])
    for k in chunks:
        part = grads_part(z, x, k)
        send(part, part, across, grads_crossed[k])

    y_far = {2: meet.at[0], -2: meet.at[1], 3: meet.at[2], -3: meet.at[3]}
    line_up, line_down = meet.at[4], meet.at[5]
    signal(y_far[2], y_device(-1))
    signal(y_far[-2], y_device(1))

    @pl.when((z == 1) & has_outward)
    def _():
        signal(line_up, across)
        signal(line_down, outward_device)

    @pl.when((z == 0) & has_outward)
    def _():
        signal(line_down, across)
        signal(line_up, outward_device)

    def y_rows(distance, base=0):
        owner = lax.rem(y + distance + Y_SIZE, Y_SIZE)
        return pl.ds(pl.multiple_of(base + owner * 16, 16), 16)

    half_columns = (pl.ds(0, D // 2), pl.ds(D // 2, D // 2))
    relayed, weighed, summed = receiver(), receiver(), receiver()
    for i, distance in enumerate((1, -1)):
        send(w_out.at[y_rows(4), half_columns[i]], relay.at[i], y_device(distance), relayed)
    for src, dst in weight_moves:
        send(src, dst, sibling, weighed, 1)
    for i, distance in enumerate((1, -1)):
        send(w_out.at[y_rows(distance), :], y_in.at[i], y_device(distance), summed)

    local[3].wait()
    row_at = lax.broadcasted_iota(jnp.int32, (SEQ, SEQ), 0)
    column_at = lax.broadcasted_iota(jnp.int32, (SEQ, SEQ), 1)
    documents = jnp.broadcast_to(docs[...].astype(F32), (SEQ, SEQ))
    own_document = jnp.sum(
        jnp.where(row_at == column_at, documents, 0.0), axis=-1, keepdims=True
    )
    allowed = (column_at <= row_at) & (documents == own_document)
    bias[...] = jnp.where(allowed, 0.0, -1e30)

    for i, distance in enumerate((2, -2)):
        pl.semaphore_wait(y_far[distance], 1)
        send(w_out.at[y_rows(distance), :], y_in.at[2 + i], y_device(distance), summed)
    signal(y_far[3], y_device(-1))
    signal(y_far[-3], y_device(2))

    def from_side(i):
        return (3, 1)[i]

    for k in chunks:
        wait_bytes_of(grads_all.at[z, pl.ds(0, 2), :, columns(k)], grads_near[k])
        part = grads_part(z, x_at[from_side(k % 2)], k)
        send(part, part, sides[k % 2], grads_far[k])
        if k != z_first:
            for i in range(2):
                part = grads_part(z, x_at[from_side(i)], k)
                send(part, part, across, grads_crossed[k])
        wait_bytes_of(normed_part(other_z, x, k), normed_crossed[k])
        part = normed_all.at[:, x, :, columns(k)]
        for side in sides:
            send(part, part, side, normed_near[k])

    for copy in local[4 : N_LOCAL - 1]:
        copy.wait()
    all_weights = w_in.at[pl.ds(0, 3456), :]
    wait_bytes_of(all_weights, local_sems.at[N_LOCAL - 1])
    wait_bytes_of(all_weights, weighed)
    wait_bytes_of(relay, relayed)
    for i, distance in enumerate((3, -3)):
        far[i] = w_back[y_rows(distance, c * HEAD_DIM), :]
        far[i, :, half_columns[i]] = (
            far[i, :, half_columns[i]].astype(F32) + relay[i].astype(F32)
        ).astype(BF16)
        pl.semaphore_wait(y_far[distance], 1)
        send(far.at[i], y_in.at[4 + i], y_device(distance), summed)

    wait_bytes_of(grads_part(other_z, x, z_first), grads_crossed[z_first])
    part = grads_part(other_z, x, z_first)
    crossed_near, crossed_far = receiver(), receiver()
    for side in sides:
        send(part, part, side, crossed_near)
    for k in chunks:
        wait_bytes_of(grads_part(z, x_at[2], k), grads_far[k])
        if k != z_first:
            part = grads_part(z, x_at[2], k)
            send(part, part, across, grads_crossed[k])
    for k in chunks:
        wait_bytes_of(normed_all.at[:, pl.ds(0, 2), :, columns(k)], normed_near[k])
        part = normed_all.at[:, x_at[from_side(k % 2)], :, columns(k)]
        send(part, part, sides[k % 2], normed_far[k])
        if k == 1:
            wait_bytes_of(grads_all.at[z, pl.ds(0, 2), :, columns(z_first)], crossed_near)
            part = grads_part(other_z, x_at[from_side(z_first % 2)], z_first)
            send(part, part, sides[z_first % 2], crossed_far)

    first = c == 0
    exchanged, exchanged_grads, returned = receiver(), receiver(), receiver()

    def blocks(ref, i, scale):
        part = ref[:, i * HEAD_DIM : (i + 1) * HEAD_DIM] * scale
        return part.reshape(8, ROWS, HEAD_DIM).astype(BF16)

    def pick(pair, condition):
        return jnp.where(condition, pair[0].astype(F32), pair[1].astype(F32)).astype(BF16)

    def sequence(i):
        return heads[i].astype(F32).reshape(SEQ, HEAD_DIM).astype(BF16)

    acc_in[...] = jnp.zeros_like(acc_in)
    acc_back[...] = jnp.zeros_like(acc_back)
    for k in chunks:
        wait_bytes_of(normed_all.at[:, x_at[2], :, columns(k)], normed_far[k])
        acc_in[...] += jnp.dot(
            normed_all[:, :, :, columns(k)].reshape(HALF, GW), w_in[columns(k), :],
            preferred_element_type=F32,
        )
        if k == GATHER - 1:
            queries = [blocks(acc_in, i, width_scale) for i in range(2)]
            heads_out[0] = pick(queries, ~first)
            heads_out[1] = blocks(acc_in, 2, width_scale)
            heads_out[2] = blocks(acc_in, 3, width_scale)
            send(heads_out.at[pl.ds(0, 3)], heads.at[pl.ds(0, 3), :, c], sibling, exchanged)
        if k == z_first:
            wait_bytes_of(grads_part(other_z, x_at[2], k), crossed_far)
        else:
            wait_bytes_of(grads_all.at[other_z, :, :, columns(k)], grads_crossed[k])
        acc_back[...] += lax.dot_general(
            grads_all[:, :, :, columns(k)].reshape(HALF, GW), w_back[:, columns(k)],
            CONTRACT_LAST, preferred_element_type=F32,
        )
    head_grads = [blocks(acc_back, i, out_scale) for i in range(2)]
    heads_out[3] = pick(head_grads, ~first)
    send(heads_out.at[3], heads.at[3, :, c], sibling, exchanged_grads)
    heads[0, :, c] = pick(queries, first)
    heads[1, :, c] = heads_out[1]
    heads[2, :, c] = heads_out[2]
    heads[3, :, c] = pick(head_grads, first)

    wait_bytes_of(y_in, summed)
    total = w_back[y_rows(0, c * HEAD_DIM), :].astype(F32)
    for i in range(6):
        total = total + y_in[i].astype(F32)
    totals[...] = total
    for i in range(Z_HI):
        z_out[i] = totals[i * OUTER_ROWS : (i + 1) * OUTER_ROWS, :].astype(BF16)
    line = {}

    upward, downward = receiver(), receiver()

    def line_copy(name, src, dst, step):
        line[name] = pltpu.make_async_remote_copy(
            src_ref=src, dst_ref=dst, send_sem=send_sems.at[2 if step > 0 else 3],
            recv_sem=upward if step > 0 else downward,
            device_id=z_device(step), device_id_type=MESH,
        )

    line_copy("up0", z_out.at[pl.ds(1, 3)], up_in, 1)
    line_copy("up1", up_out.at[pl.ds(0, 2)], up_in.at[pl.ds(1, 2)], 1)
    line_copy("up2", up_out.at[pl.ds(2, 1)], up_in.at[pl.ds(2, 1)], 1)
    line_copy("down3", z_out.at[pl.ds(0, 3)], down_in, -1)
    line_copy("down2", down_out.at[pl.ds(0, 2)], down_in.at[pl.ds(0, 2)], -1)
    line_copy("down1", down_out.at[pl.ds(2, 1)], down_in.at[pl.ds(0, 1)], -1)

    def at(position):
        return pl.when(zh == position)

    def line_sum(first, second):
        return (first.astype(F32) + second.astype(F32)).astype(BF16)

    @pl.when(zh < Z_HI - 1)
    def _():
        pl.semaphore_wait(line_up, 1)

    @pl.when(zh > 0)
    def _():
        pl.semaphore_wait(line_down, 1)

    @at(0)
    def _():
        line["up0"].start()

    @at(3)
    def _():
        line["down3"].start()

    wait_bytes_of(heads_out.at[pl.ds(0, 3)], exchanged)
    query, key, value = [sequence(i) for i in range(3)]
    row_blocks = [(slice(i * 128, (i + 1) * 128), (i + 1) * 128) for i in range(3)]
    all_probs = []
    for here, limit in row_blocks:
        scores = lax.dot_general(
            query[here], key[:limit], CONTRACT_LAST, preferred_element_type=F32
        )
        scores = scores * score_scale + bias[here, :limit]
        powers = jnp.exp(scores - jnp.max(scores, axis=-1, keepdims=True))
        all_probs.append(powers / jnp.sum(powers, axis=-1, keepdims=True))

    wait_bytes_of(heads_out.at[3], exchanged_grads)
    head_grad = sequence(3)
    key_parts, value_parts = [None] * 3, [None] * 3
    for i, (here, limit) in enumerate(row_blocks):
        probs = all_probs[i]
        prob_grads = lax.dot_general(
            head_grad[here], value[:limit], CONTRACT_LAST, preferred_element_type=F32
        )
        score_grads = (
            probs
            * (prob_grads - jnp.sum(probs * prob_grads, axis=-1, keepdims=True))
            * score_scale
        ).astype(BF16)
        probs_low = probs.astype(BF16)
        grad_rows[0, here] = jnp.dot(
            score_grads, key[:limit], preferred_element_type=F32
        )
        for j in range(i + 1):
            there = slice(j * 128, (j + 1) * 128)
            key_term = lax.dot_general(
                score_grads[:, there], query[here], CONTRACT_FIRST, preferred_element_type=F32
            )
            value_term = lax.dot_general(
                probs_low[:, there], head_grad[here], CONTRACT_FIRST, preferred_element_type=F32
            )
            key_parts[j] = key_term if i == j else key_parts[j] + key_term
            value_parts[j] = value_term if i == j else value_parts[j] + value_term
    for j in range(3):
        there = slice(j * 128, (j + 1) * 128)
        grad_rows[1, there] = key_parts[j]
        grad_rows[2, there] = value_parts[j]
    for i in range(3):
        back[i] = grad_rows[i].reshape(8, 2, ROWS, HEAD_DIM).astype(BF16)
    send(back.at[:, :, other_c], back_in, sibling, returned)

    @at(1)
    def _():
        line["up0"].wait_recv()
        up_out[0:2] = line_sum(z_out[2:4], up_in[1:3])
        line["up1"].start()

    @at(2)
    def _():
        line["down3"].wait_recv()
        down_out[0:2] = line_sum(z_out[0:2], down_in[0:2])
        line["down2"].start()

    wait_bytes_of(back_in, returned)

    def own_rows(i):
        return back[i, :, c].astype(F32).reshape(HALF, HEAD_DIM)

    def received_rows(i):
        return back_in[i].astype(F32).reshape(HALF, HEAD_DIM)

    query_pair = (own_rows(0), received_rows(0))
    upstream = jnp.concatenate(
        [
            jnp.where(first, query_pair[0], query_pair[1]).astype(BF16),
            jnp.where(first, query_pair[1], query_pair[0]).astype(BF16),
            (own_rows(1) + received_rows(1)).astype(BF16),
            (own_rows(2) + received_rows(2)).astype(BF16),
        ],
        axis=1,
    )

    def sum_columns(j):
        return pl.ds(j * SW, SW)

    hopped, neared, crossed = [[receiver() for _ in range(SUMS)] for _ in range(3)]
    plan = list(enumerate(SUM_PLAN))
    by_x = [(j, way) for j, (kind, way) in plan if kind == "x"]
    by_z = [(j, way) for j, (kind, way) in plan if kind == "z"]
    slot_of = {j: slot for group in (by_x, by_z) for slot, (j, _) in enumerate(group)}
    forward_slot = {0: 1, 1: 3}
    for j, (kind, way) in plan:
        term = lax.dot_general(
            upstream, w_in[sum_columns(j), :], CONTRACT_LAST, preferred_element_type=F32
        )
        terms[:, :, :, sum_columns(j)] = (
            (term * width_scale).reshape(2, 4, ROWS, SW).astype(BF16)
        )
        slot = slot_of[j]
        if kind == "z":
            part = terms.at[other_z, :, :, sum_columns(j)]
            send(part, from_z_z.at[slot], across, crossed[j], 4)
        else:
            part = terms.at[:, x_at[2], :, sum_columns(j)]
            send(part, hop_x.at[slot], sides[way], hopped[j], 5)
            part = terms.at[:, x_at[forward_slot[1 - way]], :, sum_columns(j)]
            send(part, near_x.at[slot, 0], sides[1 - way], neared[j], 5)

    def line_end():
        @at(2)
        def _():
            line["up1"].wait_recv()
            up_out[2:3] = line_sum(z_out[3:4], up_in[2:3])
            line["up2"].start()

        @at(1)
        def _():
            line["down2"].wait_recv()
            down_out[2:3] = line_sum(z_out[0:1], down_in[0:1])
            line["down1"].start()

    def over_x(j, way, stage):
        slot, forward = slot_of[j], x_at[forward_slot[way]]
        if stage == 1:
            wait_bytes_of(hop_x.at[slot], hopped[j])
            terms[:, forward, :, sum_columns(j)] = (
                terms[:, forward, :, sum_columns(j)].astype(F32) + hop_x[slot].astype(F32)
            ).astype(BF16)
            part = terms.at[:, forward, :, sum_columns(j)]
            send(part, near_x.at[slot, 1], sides[way], neared[j], 5)
        else:
            wait_bytes_of(near_x.at[slot], neared[j])
            terms[:, x, :, sum_columns(j)] = (
                terms[:, x, :, sum_columns(j)].astype(F32)
                + near_x[slot, 0].astype(F32)
                + near_x[slot, 1].astype(F32)
            ).astype(BF16)
            part = terms.at[other_z, x, :, sum_columns(j)]
            send(part, from_z_x.at[slot], across, crossed[j], 6)

    def over_z(j, way, stage):
        slot, forward = slot_of[j], x_at[forward_slot[way]]
        if stage == 1:
            wait_bytes_of(from_z_z.at[slot], crossed[j])
            terms[z, :, :, sum_columns(j)] = (
                terms[z, :, :, sum_columns(j)].astype(F32) + from_z_z[slot].astype(F32)
            ).astype(BF16)
            part = terms.at[z, x_at[2], :, sum_columns(j)]
            send(part, hop_z.at[slot], sides[way], hopped[j], 7)
            part = terms.at[z, x_at[forward_slot[1 - way]], :, sum_columns(j)]
            send(part, near_z.at[slot, 0], sides[1 - way], neared[j], 7)
        else:
            wait_bytes_of(hop_z.at[slot], hopped[j])
            terms[z, forward, :, sum_columns(j)] = (
                terms[z, forward, :, sum_columns(j)].astype(F32) + hop_z[slot].astype(F32)
            ).astype(BF16)
            part = terms.at[z, forward, :, sum_columns(j)]
            send(part, near_z.at[slot, 1], sides[way], neared[j], 7)

    for place, (stage, j) in enumerate(SUM_STEPS):
        if place == len(SUM_STEPS) // 2:
            line_end()
        kind, way = SUM_PLAN[j]
        (over_x if kind == "x" else over_z)(j, way, stage)

    @at(0)
    def _():
        line["down1"].wait_recv()
        mine[...] = z_out[0].astype(F32) + down_in[0].astype(F32)

    @at(1)
    def _():
        mine[...] = z_out[1].astype(F32) + up_in[0].astype(F32) + down_in[1].astype(F32)

    @at(2)
    def _():
        mine[...] = z_out[2].astype(F32) + up_in[1].astype(F32) + down_in[2].astype(F32)

    @at(3)
    def _():
        line["up2"].wait_recv()
        mine[...] = z_out[3].astype(F32) + up_in[2].astype(F32)

    mean = mine[...]
    mean = mean * (1.0 / N_REPLICA)
    delta = outer_params[...] - mean
    moment = 0.9 * outer_moment[...] + delta
    new_moment[...] = moment
    new_params[...] = outer_params[...] - 0.7 * (delta + 0.9 * moment)

    normed_grads = [None] * SUMS
    for slot, (j, way) in enumerate(by_x):
        wait_bytes_of(from_z_x.at[slot], crossed[j])
        normed_grads[j] = terms[z, x, :, sum_columns(j)].astype(F32) + from_z_x[slot].astype(F32)
    for slot, (j, way) in enumerate(by_z):
        wait_bytes_of(near_z.at[slot], neared[j])
        normed_grads[j] = (
            terms[z, x, :, sum_columns(j)].astype(F32)
            + near_z[slot, 0].astype(F32)
            + near_z[slot, 1].astype(F32)
        )
    scaled = jnp.concatenate(normed_grads, axis=1) * gain[...]
    centered = inputs[...].astype(F32) * inv_rms
    projected = jnp.sum(scaled * centered, axis=-1, keepdims=True) * (1.0 / D)
    input_grads[...] = (
        out_grads[...].astype(F32) + inv_rms * (scaled - centered * projected)
    ).astype(BF16)
    assert next(receivers, None) is None
    wait_bytes_of(w_in.at[pl.ds(0, 4368), :], send_sems.at[0])
    wait_bytes_of(all_weights, send_sems.at[1])
    x_columns, z_columns = pl.ds(0, len(by_x) * SW), pl.ds(0, len(by_z) * SW)
    wait_bytes_of(terms.at[0, :, :, z_columns], send_sems.at[4])
    wait_bytes_of(terms.at[:, pl.ds(0, 3), :, x_columns], send_sems.at[5])
    wait_bytes_of(terms.at[0, 0, :, x_columns], send_sems.at[6])
    wait_bytes_of(terms.at[0, pl.ds(0, 3), :, z_columns], send_sems.at[7])
    for position, names in enumerate((("up0",), ("up1", "down1"), ("up2", "down2"), ("down3",))):

        @at(position)
        def _():
            for name in names:
                line[name].wait_send()


def write_out(first, second, third, first_out, second_out, third_out, *scratch):
    held, (in_sems, out_sems) = scratch[:3], scratch[3:]
    results = (first_out, second_out, third_out)
    loads = [
        pltpu.make_async_copy(src, held[i], in_sems.at[i])
        for i, src in enumerate((first, second, third))
    ]
    stores = [
        pltpu.make_async_copy(held[i], dst.at[0], out_sems.at[i]) for i, dst in enumerate(results)
    ]
    for load in loads:
        load.start()
    for load, store in zip(loads, stores):
        load.wait()
        store.start()
    for store in stores:
        store.wait()


def on_device(
    inputs, out_grads, norm_gain, doc_ids, w_query, w_keyval, w_out, outer_params, outer_moment
):
    vmem = pl.BlockSpec(memory_space=pltpu.VMEM)
    hbm = pl.BlockSpec(memory_space=pltpu.HBM)
    anywhere = pl.BlockSpec(memory_space=pl.ANY)
    by_x = sum(kind == "x" for kind, _ in SUM_PLAN)
    by_z = SUMS - by_x
    input_grads, new_params, new_moment = pl.pallas_call(
        kernel,
        out_shape=(
            jax.ShapeDtypeStruct((ROWS, D), BF16),
            jax.ShapeDtypeStruct((OUTER_ROWS, D), F32),
            jax.ShapeDtypeStruct((OUTER_ROWS, D), F32),
        ),
        in_specs=[hbm] * 9,
        out_specs=(vmem, vmem, vmem),
        scratch_shapes=[
            pltpu.VMEM((ROWS, D), BF16),
            pltpu.VMEM((ROWS, D), BF16),
            pltpu.VMEM((1, D), F32),
            pltpu.VMEM((1, SEQ), jnp.int32),
            pltpu.VMEM((OUTER_ROWS, D), F32),
            pltpu.VMEM((OUTER_ROWS, D), F32),
            pltpu.VMEM((2, 4, ROWS, D), BF16),
            pltpu.VMEM((2, 4, ROWS, D), BF16),
            pltpu.VMEM((D, 4 * HEAD_DIM), BF16),
            pltpu.VMEM((2 * HEAD_DIM, D), BF16),
            pltpu.VMEM((SEQ, SEQ), F32),
            pltpu.VMEM((HALF, 4 * HEAD_DIM), F32),
            pltpu.VMEM((HALF, 2 * HEAD_DIM), F32),
            pltpu.VMEM((4, 8, 2, ROWS, HEAD_DIM), BF16),
            pltpu.VMEM((4, 8, ROWS, HEAD_DIM), BF16),
            pltpu.VMEM((3, 8, 2, ROWS, HEAD_DIM), BF16),
            pltpu.VMEM((3, 8, ROWS, HEAD_DIM), BF16),
            pltpu.VMEM((3, 8, ROWS, HEAD_DIM), BF16),
            pltpu.VMEM((3, SEQ, HEAD_DIM), F32),
            pltpu.VMEM((2, 4, ROWS, D), BF16),
            pltpu.VMEM((by_x, 2, ROWS, SW), BF16),
            pltpu.VMEM((by_x, 2, 2, ROWS, SW), BF16),
            pltpu.VMEM((by_z, ROWS, SW), BF16),
            pltpu.VMEM((by_z, 2, ROWS, SW), BF16),
            pltpu.VMEM((by_x, ROWS, SW), BF16),
            pltpu.VMEM((by_z, 4, ROWS, SW), BF16),
            pltpu.VMEM((16, D), F32),
            pltpu.VMEM((2, 16, D // 2), BF16),
            pltpu.VMEM((2, 16, D), BF16),
            pltpu.VMEM((6, 16, D), BF16),
            pltpu.VMEM((Z_HI, OUTER_ROWS, D), BF16),
            pltpu.VMEM((Z_HI - 1, OUTER_ROWS, D), BF16),
            pltpu.VMEM((Z_HI - 1, OUTER_ROWS, D), BF16),
            pltpu.VMEM((Z_HI - 1, OUTER_ROWS, D), BF16),
            pltpu.VMEM((Z_HI - 1, OUTER_ROWS, D), BF16),
            pltpu.VMEM((OUTER_ROWS, D), F32),
            pltpu.SemaphoreType.DMA((N_SEND,)),
            pltpu.SemaphoreType.DMA((N_RECEIVE,)),
            pltpu.SemaphoreType.DMA((N_LOCAL,)),
            pltpu.SemaphoreType.REGULAR((6,)),
        ],
        compiler_params=pltpu.CompilerParams(
            collective_id=0, has_side_effects=True, vmem_limit_bytes=63 * 2**20
        ),
        name="layer_backward",
    )(
        inputs[0], out_grads[0], norm_gain, doc_ids, w_query[0], w_keyval[0], w_out[0],
        outer_params[0], outer_moment[0],
    )
    input_grads, new_params, new_moment = pl.pallas_call(
        write_out,
        out_shape=(
            jax.ShapeDtypeStruct((1, ROWS, D), BF16),
            jax.ShapeDtypeStruct((1, OUTER_ROWS, D), F32),
            jax.ShapeDtypeStruct((1, OUTER_ROWS, D), F32),
        ),
        in_specs=[anywhere] * 3,
        out_specs=[anywhere] * 3,
        scratch_shapes=[
            pltpu.VMEM((ROWS, D), BF16),
            pltpu.VMEM((OUTER_ROWS, D), F32),
            pltpu.VMEM((OUTER_ROWS, D), F32),
            pltpu.SemaphoreType.DMA((3,)),
            pltpu.SemaphoreType.DMA((3,)),
        ],
        compiler_params=pltpu.CompilerParams(vmem_limit_bytes=63 * 2**20),
        name="write_out",
    )(input_grads, new_params, new_moment)
    return input_grads, new_params, new_moment


def solution(mesh):
    placed = (
        P("replica", "mp", None),
        P("replica", "mp", None),
        P(),
        P("replica", None),
        P("replica", None, "mp"),
        P("replica", None, "mp"),
        P("replica", "mp", None),
        P("mp", "replica", None),
        P("mp", "replica", None),
    )
    return jax.shard_map(
        on_device,
        mesh=mesh,
        in_specs=placed,
        out_specs=(P("replica", "mp", None), P("mp", "replica", None), P("mp", "replica", None)),
        check_vma=False,
    )
```
